512 devices in a mesh: pair: 32 (over y, z_lo, core), mom: 16 (over x, z_hi).
Axes of the slice: x: 4, y: 4, z: 16 (z_hi: 4, z_lo: 4; z = z_hi * 4 + z_lo), core: 2. Of those that a mesh axis runs over, the one named last changes fastest.
Arguments:
- coefficients: bfloat16 [2048, 32768], P(None, 'pair'), may hold values from -0.0625 to 0.0625
- exponent: float32 [32768], P('pair'), may hold values from 0.5 to 8
- amplitude: float32 [32768], P('pair'), may hold values from 1 to 6
- centers: float32 [3, 32768], P(None, 'pair'), may hold values from -8 to 8
- momenta: float32 [3, 3072], P(None, 'mom'), may hold values from -2.5 to 2.5
- quad_weight: float32 [3072], P('mom'), may hold values from 0.25 to 4
Outputs:
- gram_matrix: float32 [2, 2048, 2048], P(None, 'pair', 'mom')
The draws below stay inside these ranges and needn't reach their ends.
All inputs are finite; a program needn't handle non-finite values.
Results may differ from the reference program's by a relative error of at most 0.0028.
Values may be sent and summed in bfloat16 or wider, within the bound.
A program may use at most 64 MiB of HBM per device.

```python
import math
import jax
import jax.numpy as jnp
from jax import lax

M = 2048
P_SIZE = 32768
K = 3072
N_PAIR = 32


def raised(result, stream_key, source, target, shards_of, factor):
    owner, partner = [(jnp.arange(result.shape[dim]) // (result.shape[dim] // shards_of)).reshape([-1 if axis == dim else 1 for axis in range(result.ndim)]) for dim in (source, target)]
    chosen = jax.random.permutation(stream_key, shards_of)[partner]
    strong = (owner == chosen) | (owner == (partner + shards_of // 2) % shards_of)
    return jnp.where(strong, factor * result, result)


def block_levels(rng, extent, split, smallest, largest):
    factor_of = 1.0
    for dim, shards_of in split:
        heights = jax.random.uniform(jax.random.fold_in(jax.random.fold_in(rng, 6), dim), (shards_of,), jnp.float32, smallest / len(split), largest / len(split))
        factor_of = factor_of * jnp.repeat(jnp.exp(heights), extent[dim] // shards_of).reshape((-1,) + (1,) * (len(extent) - 1 - dim))
    return factor_of


def heavy_noise(key, shape, spread, limit, cuts, heavy, held_as=jnp.bfloat16):
    entries = spread * jax.random.normal(key, shape, jnp.float32)
    if cuts:
        entries = entries * block_levels(key, shape, cuts, -0.22, 0.18)
    return jnp.clip(raised(entries, jax.random.fold_in(key, 3), *heavy), -limit, limit).astype(held_as)


def setup_inputs(seed: int = 0) -> dict:
    key_list = jax.random.split(jax.random.key(seed), 7)
    return {
        "coefficients": heavy_noise(key_list[0], (M, P_SIZE), P_SIZE ** -0.5, 0.0625, ((1, 32),), (1, 0, 32, 2.75)),
        "exponent": jnp.clip(jnp.exp(math.log(8.0) - 2.7725887 * jax.random.uniform(key_list[1], (P_SIZE,), jnp.float32) ** block_levels(key_list[1], (P_SIZE,), ((0, 32),), -0.2, 0.2)), 0.5, 8.0),
        "amplitude": jnp.clip(jnp.exp(math.log(6.0) - 1.7917595 * jax.random.uniform(key_list[2], (P_SIZE,), jnp.float32) ** block_levels(key_list[2], (P_SIZE,), ((0, 32),), -0.2, 0.2)), 1.0, 6.0),
        "centers": jnp.clip(jax.random.uniform(key_list[3], (3, P_SIZE), jnp.float32, -8.0, 8.0) * block_levels(key_list[3], (3, P_SIZE), ((1, 32),), -0.4, 0.0), -8.0, 8.0),
        "momenta": jnp.clip(jax.random.uniform(key_list[4], (3, K), jnp.float32, -2.5, 2.5) * block_levels(key_list[4], (3, K), ((1, 16),), -0.4, 0.0), -2.5, 2.5),
        "quad_weight": jnp.clip(jnp.exp(math.log(4.0) - 2.7725887 * jax.random.uniform(key_list[5], (K,), jnp.float32) ** block_levels(key_list[5], (K,), ((0, 16),), -0.2, 0.2)), 0.25, 4.0),
    }


def make_integrals(exponent, amplitude, centers, momenta, quad_weight, count_all):
    squared = momenta[0] * momenta[0] + momenta[1] * momenta[1] + momenta[2] * momenta[2]
    phases = centers[0][:, None] * momenta[0][None, :] + centers[1][:, None] * momenta[1][None, :] + centers[2][:, None] * momenta[2][None, :]
    weight_root = jnp.sqrt(quad_weight / (count_all * (0.5 * squared + 0.5)))
    envelope = amplitude[:, None] * jnp.exp(-squared[None, :] / (4.0 * exponent[:, None])) * weight_root[None, :]
    return jnp.concatenate([envelope * jnp.cos(phases), -envelope * jnp.sin(phases)], axis=1).astype(jnp.bfloat16)

def gram_block(left_rows, right_rows):
    half_width = right_rows.shape[1] // 2
    swapped = jnp.concatenate([right_rows[:, half_width:], -right_rows[:, :half_width]], axis=1)
    dims = (((1,), (1,)), ((), ()))
    real_part = lax.dot_general(left_rows, right_rows, dims, preferred_element_type=jnp.float32)
    imag_part = lax.dot_general(left_rows, swapped, dims, preferred_element_type=jnp.float32)
    return jnp.stack([real_part, imag_part])

def reference(coefficients, exponent, amplitude, centers, momenta, quad_weight):
    block_size = P_SIZE // N_PAIR
    coef_blocks = coefficients.reshape(M, N_PAIR, block_size).transpose(1, 0, 2)
    expo_blocks = exponent.reshape(N_PAIR, block_size)
    amp_blocks = amplitude.reshape(N_PAIR, block_size)
    center_blocks = centers.reshape(3, N_PAIR, block_size).transpose(1, 0, 2)
    count_all = float(K)

    def accumulate(running, pieces):
        coef_part, expo_part, amp_part, center_part = pieces
        integ = make_integrals(expo_part, amp_part, center_part, momenta, quad_weight, count_all)
        term = jnp.dot(coef_part, integ, preferred_element_type=jnp.float32)
        return (running + term, None)
    start_value = jnp.zeros((M, 2 * K), jnp.float32)
    projected, _ = lax.scan(accumulate, start_value, (coef_blocks, expo_blocks, amp_blocks, center_blocks))
    rounded = projected.astype(jnp.bfloat16)
    return gram_block(rounded, rounded)
```

```python
import math

import jax
import jax.numpy as jnp
from jax import lax
from jax.experimental import pallas as pl
from jax.experimental.pallas import tpu as pltpu
from jax.sharding import PartitionSpec as P

MESH = pl.DeviceIdType.MESH
BF16, F32 = jnp.bfloat16, jnp.float32
NT = (((1,), (1,)), ((), ()))

RING = (2, 1, 3)


def _fit(values, degree):
    import numpy as np

    nodes = 0.125 * (1.0 - np.cos(np.pi * (np.arange(400) + 0.5) / 400))
    weights = np.polynomial.chebyshev.chebfit(8.0 * nodes - 1.0, values(nodes), degree)
    series = np.polynomial.Chebyshev(weights, domain=[0.0, 0.25])
    return [float(c) for c in series.convert(kind=np.polynomial.Polynomial).coef]


def _sin_over(v):
    import numpy as np

    u = np.sqrt(v)
    return 2.0 * np.sin(np.pi * u) / u


def _cos_of(v):
    import numpy as np

    return np.cos(np.pi * np.sqrt(v))


SIN_C = _fit(_sin_over, 4)
COS_C = _fit(_cos_of, 5)


def horner(coefs, v):
    total = coefs[-1] * v + coefs[-2]
    for c in coefs[-3::-1]:
        total = total * v + c
    return total


def encode(x):
    return (x * jnp.abs(x)).astype(BF16)


def decode(y):
    y = y.astype(F32)
    return y * lax.rsqrt(jnp.maximum(jnp.abs(y), 1e-37))


def kernel(
    coef_h, expo_h, amp_h, cen_h, mom_h, qw_h, out,
    coef_v, expo_v, amp_v, cen_v, mom_v, qw_v, rows_v, cols_v, integ,
    prod, core_s, core_r, y_s, y_own, y_r, z_s, z_r, r_own, b_all, a_all,
    x_s, x_own, x_r, g_s, g_r,
    in_sem, coef_sem, s1, s2, s3,
    core_ss, core_rs, y_ss, y_rs, z_ss, z_rs, yb_ss, yb_rs, cb_ss, cb_rs, za_ss, za_rs,
    x_ss, x_rs, g_ss, g_rs,
):
    pair, mom = lax.axis_index("pair"), lax.axis_index("mom")
    y, zl, c = pair // 8, (pair // 2) % 4, pair % 2
    x, zh = mom // 4, mom % 4
    z = zh * 4 + zl

    def dev(y=y, zl=zl, c=c, x=x, zh=zh):
        return {"pair": y * 8 + zl * 2 + c, "mom": x * 4 + zh}

    def at_z(step):
        far = (z + step + 16) % 16
        return dev(zl=far % 4, zh=far // 4)

    def send(src, dst, ss, rs, to):
        copy = pltpu.make_async_remote_copy(
            src_ref=src, dst_ref=dst, send_sem=ss, recv_sem=rs, device_id=to, device_id_type=MESH
        )
        copy.start()
        return copy

    small = [
        pltpu.make_async_copy(h, v, in_sem.at[i])
        for i, (h, v) in enumerate(
            [(expo_h, expo_v), (amp_h, amp_v), (cen_h, cen_v), (mom_h, mom_v), (qw_h, qw_v)]
        )
    ]
    for copy in small:
        copy.start()
    coef_in = []
    for t in range(4):
        copy = pltpu.make_async_copy(coef_h.at[:, (zl + 1 + t) % 4], coef_v.at[t], coef_sem.at[t])
        copy.start()
        coef_in.append(copy)

    barrier = pltpu.get_barrier_semaphore()
    near = [dev(c=1 - c)]
    near += [dev(y=(y + d) % 4) for d in RING]
    near += [dev(zl=(zl + d) % 4) for d in (1, 2, 3)]
    near += [dev(x=(x + d) % 4) for d in RING]
    near += [at_z(1), at_z(-1)]
    for to in near:
        pl.semaphore_signal(barrier, inc=1, device_id=to, device_id_type=MESH)

    for copy in small:
        copy.wait()
    m = mom_v[...]
    squared = m[0:1] * m[0:1] + m[1:2] * m[1:2] + m[2:3] * m[2:3]
    rows_v[...] = jnp.zeros_like(rows_v)
    rows_v[0:3, 0:192] = m
    rows_v[3:4, 0:192] = squared
    rows_v[4:5, 0:192] = jnp.sqrt(qw_v[...] / (3072.0 * (0.5 * squared + 0.5)))
    cols_v[...] = jnp.transpose(rows_v[...])
    cen_v[...] = cen_v[...] * (0.5 / math.pi)
    expo_v[...] = (-0.25 / math.log(2.0)) / expo_v[...]

    def integrals(i, carry):
        base = pl.multiple_of(i * 16, 16)
        k = cols_v[pl.ds(base, 16), :]
        turns = cen_v[0:1] * k[:, 0:1] + cen_v[1:2] * k[:, 1:2] + cen_v[2:3] * k[:, 2:3]
        u = turns - jnp.floor(turns + 0.5)
        v = u * u
        s = horner(SIN_C, v) * u
        envelope = (amp_v[...] * jnp.exp2(k[:, 3:4] * expo_v[...])) * k[:, 4:5]
        cosine = envelope - (0.5 * envelope) * (s * s)
        sine = (envelope * s) * horner(COS_C, v)
        first = i < 8
        row_c = pl.multiple_of(jnp.where(first, base, base + 128), 16)
        row_s = pl.multiple_of(jnp.where(first, base + 128, base + 192), 16)
        integ[pl.ds(row_c, 16), :] = cosine.astype(BF16)
        integ[pl.ds(row_s, 16), :] = (-sine).astype(BF16)
        return carry

    lax.fori_loop(0, 12, integrals, 0)

    core_c, y_c, z_c = [], [], []

    def contract(t):
        coef_in[t].wait()
        prod[t] = lax.dot_general(
            coef_v[t].reshape(512, 1024), integ[...], NT, preferred_element_type=F32
        ).reshape(4, 2, 64, 384)
        core_s[t] = encode(prod[t, :, 1 - c])
        if t == 0:
            pl.semaphore_wait(barrier, len(near))
        core_c.append(send(core_s.at[t], core_r.at[t], core_ss.at[t], core_rs.at[t], dev(c=1 - c)))

    def spread(t):
        core_c[t].wait_recv()
        total = prod[t, :, c] + decode(core_r[t])
        y_s[t] = encode(total)
        prod[t, :, c] = total
        y_own[t] = prod[t, y, c]
        y_c.append(
            [
                send(y_s.at[t, (y + d) % 4], y_r.at[t, i], y_ss.at[t, i], y_rs.at[t, i], dev(y=(y + d) % 4))
                for i, d in enumerate(RING)
            ]
        )

    contract(0)
    contract(1)
    for t in range(4):
        spread(t)
        if t < 2:
            contract(t + 2)
        if t == 1:
            for step in (1, -1):
                pl.semaphore_signal(s1, inc=1, device_id=at_z(step), device_id_type=MESH)

    for t in range(4):
        for copy in y_c[t]:
            copy.wait_recv()
        total = y_own[t]
        for i in range(3):
            total = total + decode(y_r[t, i])
        if t < 3:
            z_s[t] = encode(total)
            z_c.append(send(z_s.at[t], z_r.at[t], z_ss.at[t], z_rs.at[t], dev(zl=(zl + 1 + t) % 4)))
        if t == 0:
            pl.semaphore_wait(s1, 2)
            for step in (2, -2):
                pl.semaphore_signal(s2, inc=1, device_id=at_z(step), device_id_type=MESH)
    for t in range(3):
        z_c[t].wait_recv()
        total = total + decode(z_r[t])
    r_own[...] = total.astype(BF16)

    yb = [
        send(r_own, b_all.at[y, c], yb_ss.at[i], yb_rs.at[i], dev(y=(y + d) % 4)) for i, d in enumerate((1, 3, 2))
    ]
    za = [
        send(r_own, a_all.at[zl], za_ss.at[i], za_rs.at[i], dev(zl=(zl + d) % 4)) for i, d in enumerate((1, 3, 2))
    ]
    cb = [send(r_own, b_all.at[y, c], cb_ss.at[0], cb_rs.at[0], dev(c=1 - c))]
    b_all[y, c] = r_own[...]
    a_all[zl] = r_own[...]
    pl.semaphore_wait(s2, 2)
    for step in (4, -4):
        pl.semaphore_signal(s3, inc=1, device_id=at_z(step), device_id_type=MESH)
    for i, d in enumerate((1, 3, 2)):
        yb[i].wait_recv()
        here = b_all.at[(y + 4 - d) % 4, c]
        cb.append(send(here, here, cb_ss.at[i + 1], cb_rs.at[i + 1], dev(c=1 - c)))
    for copy in cb:
        copy.wait_recv()

    lane = lax.broadcasted_iota(jnp.int32, (64, 128), 1)
    sign = jnp.where(lane < 64, -1.0, 1.0).astype(F32)
    x_c, g_c = [], []
    for i, d in enumerate((0, 1, 3, 2)):
        r = (zl + 4 - d) % 4
        if d:
            za[i - 1].wait_recv()
        rows = a_all[r].astype(F32)
        turned = jnp.concatenate(
            [-rows[:, 128:256], rows[:, 0:128], pltpu.roll(rows[:, 256:384], 64, 1) * sign], axis=1
        )
        left = (jnp.concatenate([rows, turned], axis=0) * 2.0**32).astype(BF16)
        for n in range(4):
            block = lax.dot_general(left, b_all[n].reshape(128, 384), NT, preferred_element_type=F32)
            x_own[i, n] = block
            x_s[i, n] = encode(block)
        x_c.append(
            [
                send(x_s.at[i, (x + e) % 4], x_r.at[i, j], x_ss.at[i, j], x_rs.at[i, j], dev(x=(x + e) % 4))
                for j, e in enumerate(RING)
            ]
        )

    pl.semaphore_wait(s3, 2)
    for i, d in enumerate((0, 1, 3, 2)):
        r = (zl + 4 - d) % 4
        for copy in x_c[i]:
            copy.wait_recv()
        total = x_own[i, x]
        for j in range(3):
            total = total + decode(x_r[i, j])
        g_s[i] = encode(total)
        here = jnp.logical_and(r == zl, zh == zl)

        @pl.when(here)
        def _():
            g_r[zh] = g_s[i]

        @pl.when(jnp.logical_not(here))
        def _():
            send(g_s.at[i], g_r.at[zh], g_ss.at[i], g_rs.at[zh], dev(zl=r, zh=zl))

    total = jnp.zeros((128, 128), F32)
    for a in range(4):
        here = jnp.logical_and(zl == zh, zh == a)

        @pl.when(jnp.logical_not(here))
        def _():
            pltpu.make_async_remote_copy(
                src_ref=g_s.at[0], dst_ref=g_r.at[a], send_sem=g_ss.at[0], recv_sem=g_rs.at[a],
                device_id=dev(zl=zh, zh=a), device_id_type=MESH,
            ).wait_recv()

        total = total + decode(g_r[a])
    out[...] = (total * (2.0**-32)).reshape(2, 64, 128)

    for copy in core_c + [k for group in y_c for k in group] + z_c + yb + za + cb + [k for group in x_c for k in group]:
        copy.wait_send()
    for i, d in enumerate((0, 1, 3, 2)):
        r = (zl + 4 - d) % 4

        @pl.when(jnp.logical_not(jnp.logical_and(r == zl, zh == zl)))
        def _():
            pltpu.make_async_remote_copy(
                src_ref=g_s.at[i], dst_ref=g_r.at[0], send_sem=g_ss.at[i], recv_sem=g_rs.at[0],
                device_id=dev(zl=r, zh=zl), device_id_type=MESH,
            ).wait_send()


def per_device(coefficients, exponent, amplitude, centers, momenta, quad_weight):
    vmem, dma = pltpu.VMEM, pltpu.SemaphoreType.DMA
    regular = pltpu.SemaphoreType.REGULAR
    return pl.pallas_call(
        kernel,
        out_shape=jax.ShapeDtypeStruct((2, 64, 128), F32),
        in_specs=[pl.BlockSpec(memory_space=pl.ANY)] * 6,
        out_specs=pl.BlockSpec(memory_space=pltpu.VMEM),
        scratch_shapes=[
            vmem((4, 4, 128, 1024), BF16), vmem((1, 1024), F32), vmem((1, 1024), F32), vmem((3, 1024), F32),
            vmem((3, 192), F32), vmem((1, 192), F32), vmem((8, 256), F32), vmem((256, 8), F32),
            vmem((384, 1024), BF16),
            vmem((4, 4, 2, 64, 384), F32), vmem((4, 4, 64, 384), BF16), vmem((4, 4, 64, 384), BF16),
            vmem((4, 4, 64, 384), BF16), vmem((4, 64, 384), F32), vmem((4, 3, 64, 384), BF16),
            vmem((3, 64, 384), BF16), vmem((3, 64, 384), BF16), vmem((64, 384), BF16),
            vmem((4, 2, 64, 384), BF16), vmem((4, 64, 384), BF16),
            vmem((4, 4, 128, 128), BF16), vmem((4, 4, 128, 128), F32), vmem((4, 3, 128, 128), BF16),
            vmem((4, 128, 128), BF16), vmem((4, 128, 128), BF16),
            dma((5,)), dma((4,)), regular, regular, regular,
            dma((4,)), dma((4,)), dma((4, 3)), dma((4, 3)), dma((3,)), dma((3,)),
            dma((3,)), dma((3,)), dma((4,)), dma((4,)), dma((3,)), dma((3,)),
            dma((4, 3)), dma((4, 3)), dma((4,)), dma((4,)),
        ],
        compiler_params=pltpu.CompilerParams(
            collective_id=0, has_side_effects=True, vmem_limit_bytes=48 * 1024 * 1024
        ),
        name="scattering",
    )(
        coefficients.reshape(4, 4, 128, 1024),
        exponent.reshape(1, 1024),
        amplitude.reshape(1, 1024),
        centers,
        momenta,
        quad_weight.reshape(1, 192),
    )


def solution(mesh):
    return jax.shard_map(
        per_device,
        mesh=mesh,
        in_specs=(P(None, "pair"), P("pair"), P("pair"), P(None, "pair"), P(None, "mom"), P("mom")),
        out_specs=P(None, "pair", "mom"),
        check_vma=False,
    )
```

```python
import math

import jax
import jax.numpy as jnp
from jax import lax
from jax.experimental import pallas as pl
from jax.experimental.pallas import tpu as pltpu
from jax.sharding import PartitionSpec as P

MESH = pl.DeviceIdType.MESH
scope = jax.named_scope
BF16, F32 = jnp.bfloat16, jnp.float32
NT = (((1,), (1,)), ((), ()))

RING = (2, 1, 3)
LINE = (1, 3, 2, 0)


def _fit(values, degree):
    import numpy as np

    nodes = 0.125 * (1.0 - np.cos(np.pi * (np.arange(400) + 0.5) / 400))
    weights = np.polynomial.chebyshev.chebfit(8.0 * nodes - 1.0, values(nodes), degree)
    series = np.polynomial.Chebyshev(weights, domain=[0.0, 0.25])
    return [float(c) for c in series.convert(kind=np.polynomial.Polynomial).coef]


def _sin_over(v):
    import numpy as np

    u = np.sqrt(v)
    return 2.0 * np.sin(np.pi * u) / u


def _cos_of(v):
    import numpy as np

    return np.cos(np.pi * np.sqrt(v))


SIN_C = _fit(_sin_over, 4)
COS_C = _fit(_cos_of, 5)


def horner(coefs, v):
    total = coefs[-1] * v + coefs[-2]
    for c in coefs[-3::-1]:
        total = total * v + c
    return total


def encode(x):
    return (x * jnp.abs(x)).astype(BF16)


def decode(y):
    y = y.astype(F32)
    return y * lax.rsqrt(jnp.maximum(jnp.abs(y), 1e-37))


def kernel(
    coef_h, expo_h, amp_h, cen_h, mom_h, qw_h, out,
    coef_v, expo_v, amp_v, cen_v, mom_v, qw_v, rows_v, cols_v, integ,
    prod, core_s, core_r, y_s, y_r, z_s, z_r, r_own, b_all, a_all,
    x_s, x_own, x_r, g_s, g_r,
    in_sem, coef_sem, s1, s2, s3,
    core_ss, core_rs, y_ss, y_rs, z_ss, z_rs, yb_ss, yb_rs, cb_ss, cb_rs, za_ss, za_rs,
    x_ss, x_rs, g_ss, g_rs,
):
    pair, mom = lax.axis_index("pair"), lax.axis_index("mom")
    y, zl, c = pair // 8, (pair // 2) % 4, pair % 2
    x, zh = mom // 4, mom % 4
    z = zh * 4 + zl

    def label(zl):
        step = 3 - 3 * zl + 5 * (zl * (zl - 1) // 2) - 8 * (zl * (zl - 1) * (zl - 2) // 6)
        return (zh + step) % 4

    def holder(group, window):
        o = (group - window + 4) % 4
        return 1 + 2 * o - 3 * (o * (o - 1) // 2) + 2 * (o * (o - 1) * (o - 2) // 6)

    group = label(zl)

    def dev(y=y, zl=zl, c=c, x=x, zh=zh):
        return {"pair": y * 8 + zl * 2 + c, "mom": x * 4 + zh}

    def at_z(step):
        far = (z + step + 16) % 16
        return dev(zl=far % 4, zh=far // 4)

    def send(src, dst, ss, rs, to):
        copy = pltpu.make_async_remote_copy(
            src_ref=src, dst_ref=dst, send_sem=ss, recv_sem=rs, device_id=to, device_id_type=MESH
        )
        copy.start()
        return copy

    small = [
        pltpu.make_async_copy(h, v, in_sem.at[i])
        for i, (h, v) in enumerate(
            [(expo_h, expo_v), (amp_h, amp_v), (cen_h, cen_v), (mom_h, mom_v), (qw_h, qw_v)]
        )
    ]
    for copy in small:
        copy.start()
    coef_in = []
    for t in range(4):
        copy = pltpu.make_async_copy(coef_h.at[:, label((zl + LINE[t]) % 4)], coef_v.at[t], coef_sem.at[t])
        copy.start()
        coef_in.append(copy)

    barrier = pltpu.get_barrier_semaphore()
    near = [dev(c=1 - c)]
    near += [dev(y=(y + d) % 4) for d in RING]
    near += [dev(zl=(zl + d) % 4) for d in (1, 2, 3)]
    near += [dev(x=(x + d) % 4) for d in RING]
    near += [at_z(1), at_z(-1)]
    for to in near:
        pl.semaphore_signal(barrier, inc=1, device_id=to, device_id_type=MESH)

    with scope("small_wait"):
        for copy in small:
            copy.wait()
    m = mom_v[...]
    squared = m[0:1] * m[0:1] + m[1:2] * m[1:2] + m[2:3] * m[2:3]
    rows_v[...] = jnp.zeros_like(rows_v)
    rows_v[0:3, 0:192] = m
    rows_v[3:4, 0:192] = squared
    rows_v[4:5, 0:192] = jnp.sqrt(qw_v[...] / (3072.0 * (0.5 * squared + 0.5)))
    cols_v[...] = jnp.transpose(rows_v[...])
    cen_v[...] = cen_v[...] * (0.5 / math.pi)
    expo_v[...] = (-0.25 / math.log(2.0)) / expo_v[...]

    def integrals(i, carry):
        base = pl.multiple_of(i * 16, 16)
        k = cols_v[pl.ds(base, 16), :]
        turns = cen_v[0:1] * k[:, 0:1] + cen_v[1:2] * k[:, 1:2] + cen_v[2:3] * k[:, 2:3]
        u = turns - jnp.floor(turns + 0.5)
        v = u * u
        s = horner(SIN_C, v) * u
        envelope = (amp_v[...] * jnp.exp2(k[:, 3:4] * expo_v[...])) * k[:, 4:5]
        cosine = envelope - (0.5 * envelope) * (s * s)
        sine = (envelope * s) * horner(COS_C, v)
        first = i < 8
        row_c = pl.multiple_of(jnp.where(first, base, base + 128), 16)
        row_s = pl.multiple_of(jnp.where(first, base + 128, base + 192), 16)
        integ[pl.ds(row_c, 16), :] = cosine.astype(BF16)
        integ[pl.ds(row_s, 16), :] = (-sine).astype(BF16)
        return carry

    with scope("integrals"):
        lax.fori_loop(0, 12, integrals, 0)

    core_c, y_c, z_c = [], [], []

    def half(t, core):
        rows = coef_v[t, :, core].reshape(256, 1024)
        return lax.dot_general(rows, integ[...], NT, preferred_element_type=F32).reshape(4, 64, 384)

    def contract(t):
        with scope(f"coef_wait{t}"):
            coef_in[t].wait()
        core_s[t] = encode(half(t, 1 - c))
        if t == 0:
            with scope("barrier"):
                pl.semaphore_wait(barrier, len(near))
        core_c.append(send(core_s.at[t], core_r.at[t], core_ss.at[t], core_rs.at[t], dev(c=1 - c)))
        prod[t] = half(t, c)

    def spread(t):
        with scope(f"core_wait{t}"):
            core_c[t].wait_recv()
        total = prod[t] + decode(core_r[t])
        y_s[t] = encode(total)
        prod[t] = total
        y_c.append(
            [
                send(y_s.at[t, (y + d) % 4], y_r.at[t, i], y_ss.at[t, i], y_rs.at[t, i], dev(y=(y + d) % 4))
                for i, d in enumerate(RING)
            ]
        )

    contract(0)
    contract(1)
    for t in range(4):
        spread(t)
        if t < 2:
            contract(t + 2)
        if t == 1:
            for step in (1, -1):
                pl.semaphore_signal(s1, inc=1, device_id=at_z(step), device_id_type=MESH)

    for t in range(4):
        with scope(f"y_wait{t}"):
            for copy in y_c[t]:
                copy.wait_recv()
        total = prod[t, y]
        for i in range(3):
            total = total + decode(y_r[t, i])
        if t < 3:
            z_s[t] = encode(total)
            z_c.append(send(z_s.at[t], z_r.at[t], z_ss.at[t], z_rs.at[t], dev(zl=(zl + LINE[t]) % 4)))
        if t == 0:
            pl.semaphore_wait(s1, 2)
            for step in (2, -2):
                pl.semaphore_signal(s2, inc=1, device_id=at_z(step), device_id_type=MESH)
    for t in range(3):
        with scope(f"z_wait{t}"):
            z_c[t].wait_recv()
        total = total + decode(z_r[t])
    r_own[...] = total.astype(BF16)

    yb = [
        send(r_own, b_all.at[y, c], yb_ss.at[i], yb_rs.at[i], dev(y=(y + d) % 4)) for i, d in enumerate((1, 3, 2))
    ]
    za = [
        send(r_own, a_all.at[group], za_ss.at[i], za_rs.at[i], dev(zl=(zl + d) % 4)) for i, d in enumerate((1, 3, 2))
    ]
    cb = [send(r_own, b_all.at[y, c], cb_ss.at[0], cb_rs.at[0], dev(c=1 - c))]
    b_all[y, c] = r_own[...]
    a_all[group] = r_own[...]
    pl.semaphore_wait(s2, 2)
    for step in (4, -4):
        pl.semaphore_signal(s3, inc=1, device_id=at_z(step), device_id_type=MESH)
    for i, d in enumerate((1, 3, 2)):
        with scope(f"yb_wait{i}"):
            yb[i].wait_recv()
        here = b_all.at[(y + 4 - d) % 4, c]
        cb.append(send(here, here, cb_ss.at[i + 1], cb_rs.at[i + 1], dev(c=1 - c)))
    with scope("cb_wait"):
        for copy in cb:
            copy.wait_recv()

    lane = lax.broadcasted_iota(jnp.int32, (64, 128), 1)
    sign = jnp.where(lane < 64, -1.0, 1.0).astype(F32)
    x_c, g_c = [], []
    for i, d in enumerate((0, 1, 3, 2)):
        r = label((zl + 4 - d) % 4)
        if d:
            with scope(f"za_wait{i}"):
                za[i - 1].wait_recv()
        rows = a_all[r].astype(F32)
        turned = jnp.concatenate(
            [-rows[:, 128:256], rows[:, 0:128], pltpu.roll(rows[:, 256:384], 64, 1) * sign], axis=1
        )
        left = (jnp.concatenate([rows, turned], axis=0) * 2.0**32).astype(BF16)
        for n in range(4):
            block = lax.dot_general(left, b_all[n].reshape(128, 384), NT, preferred_element_type=F32)
            x_own[i, n] = block
            x_s[i, n] = encode(block)
        x_c.append(
            [
                send(x_s.at[i, (x + e) % 4], x_r.at[i, j], x_ss.at[i, j], x_rs.at[i, j], dev(x=(x + e) % 4))
                for j, e in enumerate(RING)
            ]
        )

    with scope("s3_wait"):
        pl.semaphore_wait(s3, 2)
    for i, d in enumerate((0, 1, 3, 2)):
        r = label((zl + 4 - d) % 4)
        with scope(f"x_wait{i}"):
            for copy in x_c[i]:
                copy.wait_recv()
        total = x_own[i, x]
        for j in range(3):
            total = total + decode(x_r[i, j])
        g_s[i] = encode(total)
        here = jnp.logical_and(r == zl, zh == group)

        @pl.when(here)
        def _():
            g_r[zh] = g_s[i]

        @pl.when(jnp.logical_not(here))
        def _():
            send(g_s.at[i], g_r.at[zh], g_ss.at[i], g_rs.at[zh], dev(zl=r, zh=group))

    total = jnp.zeros((128, 128), F32)
    for a in range(4):
        source = holder(zh, a)
        here = jnp.logical_and(source == zl, zh == a)

        @pl.when(jnp.logical_not(here))
        def _():
            with scope(f"g_wait{a}"):
                pltpu.make_async_remote_copy(
                    src_ref=g_s.at[0], dst_ref=g_r.at[a], send_sem=g_ss.at[0], recv_sem=g_rs.at[a],
                    device_id=dev(zl=source, zh=a), device_id_type=MESH,
                ).wait_recv()

        total = total + decode(g_r[a])
    out[...] = (total * (2.0**-32)).reshape(2, 64, 128)

    for copy in core_c + [k for group in y_c for k in group] + z_c + yb + za + cb + [k for group in x_c for k in group]:
        copy.wait_send()
    for i, d in enumerate((0, 1, 3, 2)):
        r = label((zl + 4 - d) % 4)

        @pl.when(jnp.logical_not(jnp.logical_and(r == zl, zh == group)))
        def _():
            pltpu.make_async_remote_copy(
                src_ref=g_s.at[i], dst_ref=g_r.at[0], send_sem=g_ss.at[i], recv_sem=g_rs.at[0],
                device_id=dev(zl=r, zh=group), device_id_type=MESH,
            ).wait_send()


def per_device(coefficients, exponent, amplitude, centers, momenta, quad_weight):
    vmem, dma = pltpu.VMEM, pltpu.SemaphoreType.DMA
    regular = pltpu.SemaphoreType.REGULAR
    return pl.pallas_call(
        kernel,
        out_shape=jax.ShapeDtypeStruct((2, 64, 128), F32),
        in_specs=[pl.BlockSpec(memory_space=pl.ANY)] * 6,
        out_specs=pl.BlockSpec(memory_space=pltpu.VMEM),
        scratch_shapes=[
            vmem((4, 4, 2, 64, 1024), BF16), vmem((1, 1024), F32), vmem((1, 1024), F32), vmem((3, 1024), F32),
            vmem((3, 192), F32), vmem((1, 192), F32), vmem((8, 256), F32), vmem((256, 8), F32),
            vmem((384, 1024), BF16),
            vmem((4, 4, 64, 384), F32), vmem((4, 4, 64, 384), BF16), vmem((4, 4, 64, 384), BF16),
            vmem((4, 4, 64, 384), BF16), vmem((4, 3, 64, 384), BF16),
            vmem((3, 64, 384), BF16), vmem((3, 64, 384), BF16), vmem((64, 384), BF16),
            vmem((4, 2, 64, 384), BF16), vmem((4, 64, 384), BF16),
            vmem((4, 4, 128, 128), BF16), vmem((4, 4, 128, 128), F32), vmem((4, 3, 128, 128), BF16),
            vmem((4, 128, 128), BF16), vmem((4, 128, 128), BF16),
            dma((5,)), dma((4,)), regular, regular, regular,
            dma((4,)), dma((4,)), dma((4, 3)), dma((4, 3)), dma((3,)), dma((3,)),
            dma((3,)), dma((3,)), dma((4,)), dma((4,)), dma((3,)), dma((3,)),
            dma((4, 3)), dma((4, 3)), dma((4,)), dma((4,)),
        ],
        compiler_params=pltpu.CompilerParams(
            collective_id=0, has_side_effects=True, vmem_limit_bytes=60 * 1024 * 1024
        ),
        name="scattering",
    )(
        coefficients.reshape(4, 4, 2, 64, 1024),
        exponent.reshape(1, 1024),
        amplitude.reshape(1, 1024),
        centers,
        momenta,
        quad_weight.reshape(1, 192),
    )


def solution(mesh):
    return jax.shard_map(
        per_device,
        mesh=mesh,
        in_specs=(P(None, "pair"), P("pair"), P("pair"), P(None, "pair"), P(None, "mom"), P("mom")),
        out_specs=P(None, "pair", "mom"),
        check_vma=False,
    )
```

```python
import math

import jax
import jax.numpy as jnp
from jax import lax
from jax.experimental import pallas as pl
from jax.experimental.pallas import tpu as pltpu
from jax.sharding import PartitionSpec as P

MESH = pl.DeviceIdType.MESH
scope = jax.named_scope
BF16, F32 = jnp.bfloat16, jnp.float32
NT = (((1,), (1,)), ((), ()))

RING = (2, 1, 3)
NEAR = (1, 3, 2)
LINE = (2, 1, 3, 0)


def _fit(values, degree):
    import numpy as np

    nodes = 0.125 * (1.0 - np.cos(np.pi * (np.arange(400) + 0.5) / 400))
    weights = np.polynomial.chebyshev.chebfit(8.0 * nodes - 1.0, values(nodes), degree)
    series = np.polynomial.Chebyshev(weights, domain=[0.0, 0.25])
    return [float(c) for c in series.convert(kind=np.polynomial.Polynomial).coef]


def _sin_over(v):
    import numpy as np

    u = np.sqrt(v)
    return 2.0 * np.sin(np.pi * u) / u


def _cos_of(v):
    import numpy as np

    return np.cos(np.pi * np.sqrt(v))


SIN_C = _fit(_sin_over, 4)
COS_C = _fit(_cos_of, 5)


def horner(coefs, v):
    total = coefs[-1] * v + coefs[-2]
    for c in coefs[-3::-1]:
        total = total * v + c
    return total


def encode(x):
    return (x * jnp.abs(x)).astype(BF16)


def decode(y):
    y = y.astype(F32)
    return y * lax.rsqrt(jnp.maximum(jnp.abs(y), 1e-37))


def kernel(
    coef_h, expo_h, amp_h, cen_h, mom_h, qw_h, out,
    coef_v, expo_v, amp_v, cen_v, mom_v, qw_v, rows_v, cols_v, integ,
    prod, core_s, core_r, y_s, y_r, z_s, z_r, r_own, b_all, a_all,
    x_s, x_own, x_r, g_s, g_r,
    in_sem, coef_sem, s1, s2, s3,
    core_ss, core_rs, y_ss, y_rs, z_ss, z_rs, ca_ss, ca_rs, yb_ss, yb_rs, za_ss, za_rs,
    x_ss, x_rs, g_ss, g_rs,
):
    pair, mom = lax.axis_index("pair"), lax.axis_index("mom")
    y, zl, c = pair // 8, (pair // 2) % 4, pair % 2
    x, zh = mom // 4, mom % 4
    z = zh * 4 + zl

    def label(zl):
        step = 3 - zl - zl * (zl - 1) // 2 + 4 * (zl * (zl - 1) * (zl - 2) // 6)
        return (zh + step) % 4

    def holder(group, window):
        o = (group - window + 4) % 4
        return 2 + o - 3 * (o * (o - 1) // 2) + 4 * (o * (o - 1) * (o - 2) // 6)

    group = label(zl)

    def dev(y=y, zl=zl, c=c, x=x, zh=zh):
        return {"pair": y * 8 + zl * 2 + c, "mom": x * 4 + zh}

    def at_z(step, c=c):
        far = (z + step + 16) % 16
        return dev(zl=far % 4, c=c, zh=far // 4)

    def send(src, dst, ss, rs, to):
        copy = pltpu.make_async_remote_copy(
            src_ref=src, dst_ref=dst, send_sem=ss, recv_sem=rs, device_id=to, device_id_type=MESH
        )
        copy.start()
        return copy

    small = [
        pltpu.make_async_copy(h, v, in_sem.at[i])
        for i, (h, v) in enumerate(
            [(expo_h, expo_v), (amp_h, amp_v), (cen_h, cen_v), (mom_h, mom_v), (qw_h, qw_v)]
        )
    ]
    for copy in small:
        copy.start()
    barrier = pltpu.get_barrier_semaphore()
    near = [dev(c=1 - c)]
    near += [dev(y=(y + d) % 4) for d in RING]
    near += [dev(zl=(zl + d) % 4) for d in (1, 2, 3)]
    near += [dev(x=(x + d) % 4) for d in RING]
    near += [at_z(1), at_z(-1), at_z(1, 1 - c), at_z(-1, 1 - c)]
    for to in near:
        pl.semaphore_signal(barrier, inc=1, device_id=to, device_id_type=MESH)

    with scope("small_wait"):
        for copy in small:
            copy.wait()
    coef_in = []
    for t in range(4):
        copy = pltpu.make_async_copy(coef_h.at[:, label((zl + LINE[t]) % 4)], coef_v.at[t], coef_sem.at[t])
        copy.start()
        coef_in.append(copy)
    m = mom_v[...]
    squared = m[0:1] * m[0:1] + m[1:2] * m[1:2] + m[2:3] * m[2:3]
    rows_v[...] = jnp.zeros_like(rows_v)
    rows_v[0:3, 0:192] = m
    rows_v[3:4, 0:192] = squared
    rows_v[4:5, 0:192] = jnp.sqrt(qw_v[...] / (3072.0 * (0.5 * squared + 0.5)))
    cols_v[...] = jnp.transpose(rows_v[...])
    cen_v[...] = cen_v[...] * (0.5 / math.pi)
    expo_v[...] = (-0.25 / math.log(2.0)) / expo_v[...]

    def integrals(i, carry):
        base = pl.multiple_of(i * 16, 16)
        k = cols_v[pl.ds(base, 16), :]
        first = i < 8
        row_c = pl.multiple_of(jnp.where(first, base, base + 128), 16)
        row_s = pl.multiple_of(jnp.where(first, base + 128, base + 192), 16)
        for start in range(0, 1024, 256):
            p = slice(start, start + 256)
            turns = cen_v[0:1, p] * k[:, 0:1] + cen_v[1:2, p] * k[:, 1:2] + cen_v[2:3, p] * k[:, 2:3]
            u = turns - jnp.round(turns)
            v = u * u
            s = horner(SIN_C, v) * u
            envelope = (amp_v[:, p] * jnp.exp2(k[:, 3:4] * expo_v[:, p])) * k[:, 4:5]
            integ[pl.ds(row_c, 16), p] = (envelope - (0.5 * envelope) * (s * s)).astype(BF16)
            integ[pl.ds(row_s, 16), p] = (-((envelope * s) * horner(COS_C, v))).astype(BF16)
        return carry

    with scope("integrals"):
        lax.fori_loop(0, 12, integrals, 0, unroll=12)

    core_c, y_c, z_c = [], [], []

    def half(t, core):
        rows = coef_v[t, :, core].reshape(256, 1024)
        return lax.dot_general(rows, integ[...], NT, preferred_element_type=F32).reshape(4, 64, 384)

    def contract(t):
        with scope(f"coef_wait{t}"):
            coef_in[t].wait()
        core_s[t] = encode(half(t, 1 - c))
        if t == 0:
            with scope("barrier"):
                pl.semaphore_wait(barrier, len(near))
        core_c.append(send(core_s.at[t], core_r.at[t], core_ss.at[t], core_rs.at[t], dev(c=1 - c)))
        prod[t] = half(t, c)

    def spread(t):
        with scope(f"core_wait{t}"):
            core_c[t].wait_recv()
        total = prod[t] + decode(core_r[t])
        prod[t] = total
        y_s[t] = encode(total)
        y_c.append(
            [
                send(y_s.at[t, (y + d) % 4], y_r.at[t, i], y_ss.at[t, i], y_rs.at[t, i], dev(y=(y + d) % 4))
                for i, d in enumerate(RING)
            ]
        )

    contract(0)
    contract(1)
    for t in range(4):
        spread(t)
        if t < 2:
            contract(t + 2)
        if t == 1:
            for step in (1, -1):
                pl.semaphore_signal(s1, inc=1, device_id=at_z(step), device_id_type=MESH)

    for t in range(4):
        with scope(f"y_wait{t}"):
            for copy in y_c[t]:
                copy.wait_recv()
        total = prod[t, y]
        for i in range(3):
            total = total + decode(y_r[t, i])
        if t < 3:
            z_s[t] = encode(total)
            z_c.append(send(z_s.at[t], z_r.at[t], z_ss.at[t], z_rs.at[t], dev(zl=(zl + LINE[t]) % 4)))
        if t == 0:
            pl.semaphore_wait(s1, 2)
            for step in (2, -2):
                pl.semaphore_signal(s2, inc=1, device_id=at_z(step), device_id_type=MESH)
    for t in range(3):
        with scope(f"z_wait{t}"):
            z_c[t].wait_recv()
        total = total + decode(z_r[t])
    r_own[...] = (total * 65536.0).astype(BF16)

    ca = [send(r_own, a_all.at[group, c], ca_ss.at[0], ca_rs.at[0], dev(c=1 - c))]
    yb = [
        send(r_own, b_all.at[y, 0], yb_ss.at[i], yb_rs.at[i], dev(y=(y + d) % 4)) for i, d in enumerate(NEAR)
    ]
    za = [
        send(r_own, a_all.at[group, c], za_ss.at[i], za_rs.at[i], dev(zl=(zl + d) % 4)) for i, d in enumerate(NEAR)
    ]
    lane = lax.broadcasted_iota(jnp.int32, (64, 128), 1)

    def turn(n):
        rows = b_all[n, 0].astype(F32)
        last = pltpu.roll(rows[:, 256:384], 64, 1) * jnp.where(lane < 64, 1.0, -1.0)
        b_all[n, 1] = jnp.concatenate([rows[:, 128:256], -rows[:, 0:128], last], axis=1).astype(BF16)

    b_all[y, 0] = r_own[...]
    a_all[group, c] = r_own[...]
    pl.semaphore_wait(s2, 2)
    for step in (4, -4):
        pl.semaphore_signal(s3, inc=1, device_id=at_z(step), device_id_type=MESH)
    x_c = []
    with scope("ca_wait0"):
        ca[0].wait_recv()
    left = a_all[group].reshape(128, 384)
    def forward(i):
        with scope(f"za_wait{i}"):
            za[i].wait_recv()
        here = a_all.at[label((zl + 4 - NEAR[i]) % 4), c]
        ca.append(send(here, here, ca_ss.at[i + 1], ca_rs.at[i + 1], dev(c=1 - c)))

    for i, d in enumerate((0, *NEAR)):
        n = (y + 4 - d) % 4
        if i == 3:
            forward(0)
            forward(1)
        if d:
            with scope(f"yb_wait{i}"):
                yb[i - 1].wait_recv()
        turn(n)
        block = lax.dot_general(left, b_all[n].reshape(128, 384), NT, preferred_element_type=F32)
        x_own[0, n] = block
        x_s[0, n] = encode(block)
        e = (n - x + 4) % 4

        @pl.when(e > 0)
        def _():
            send(x_s.at[0, n], x_r.at[0, e - 1], x_ss.at[0, e - 1], x_rs.at[0, e - 1], dev(x=n))

    x_c.append(
        [
            pltpu.make_async_remote_copy(
                src_ref=x_s.at[0, 0], dst_ref=x_r.at[0, j], send_sem=x_ss.at[0, j], recv_sem=x_rs.at[0, j],
                device_id=dev(x=(x + 1) % 4), device_id_type=MESH,
            )
            for j in range(3)
        ]
    )

    def tile(i):
        with scope(f"ca_wait{i}"):
            ca[i].wait_recv()
        left = a_all[label((zl + 4 - (0, *NEAR)[i]) % 4)].reshape(128, 384)
        block = lax.dot_general(left, b_all[...].reshape(512, 384), NT, preferred_element_type=F32)
        for n in range(4):
            x_own[i, n] = block[:, n * 128 : n * 128 + 128]
            x_s[i, n] = encode(block[:, n * 128 : n * 128 + 128])
        x_c.append(
            [
                send(x_s.at[i, (x + e) % 4], x_r.at[i, j], x_ss.at[i, j], x_rs.at[i, j], dev(x=(x + e) % 4))
                for j, e in enumerate(RING)
            ]
        )

    forward(2)
    for i in range(1, 4):
        tile(i)

    with scope("s3_wait"):
        pl.semaphore_wait(s3, 2)
    for i in range(4):
        r = label((zl + 4 - (0, *NEAR)[i]) % 4)
        with scope(f"x_wait{i}"):
            for copy in x_c[i]:
                copy.wait_recv()
        total = x_own[i, x]
        for j in range(3):
            total = total + decode(x_r[i, j])
        g_s[i] = encode(total).reshape(2, 64, 128)
        for half in range(2):
            here = jnp.logical_and(jnp.logical_and(r == zl, zh == group), c == half)

            @pl.when(here)
            def _():
                g_r[zh, c] = g_s[i, half]

            @pl.when(jnp.logical_not(here))
            def _():
                send(
                    g_s.at[i, half], g_r.at[zh, c], g_ss.at[i, half], g_rs.at[zh, c],
                    dev(zl=r, c=half, zh=group),
                )

    with scope("left"):
        for copy in core_c + sum(y_c, []) + z_c + ca + yb + za + sum(x_c, []):
            copy.wait_send()

    total = [jnp.zeros((64, 128), F32)] * 2
    for a in range(4):
        source = holder(zh, a)
        for core in range(2):
            here = jnp.logical_and(jnp.logical_and(source == zl, zh == a), c == core)

            @pl.when(jnp.logical_not(here))
            def _():
                with scope(f"g_wait{a}{core}"):
                    pltpu.make_async_remote_copy(
                        src_ref=g_s.at[0, 0], dst_ref=g_r.at[a, core], send_sem=g_ss.at[0, 0],
                        recv_sem=g_rs.at[a, core], device_id=dev(zl=source, c=core, zh=a), device_id_type=MESH,
                    ).wait_recv()

            total[core] = total[core] + decode(g_r[a, core])
    first, second = total[0] * 2.0**-32, total[1] * 2.0**-32
    out[0] = jnp.where(lane < 64, first, pltpu.roll(second, 64, 1))
    out[1] = jnp.where(lane < 64, pltpu.roll(first, 64, 1), second)

    for i in range(4):
        r = label((zl + 4 - (0, *NEAR)[i]) % 4)
        for half in range(2):
            here = jnp.logical_and(jnp.logical_and(r == zl, zh == group), c == half)

            @pl.when(jnp.logical_not(here))
            def _():
                pltpu.make_async_remote_copy(
                    src_ref=g_s.at[i, half], dst_ref=g_r.at[0, 0], send_sem=g_ss.at[i, half], recv_sem=g_rs.at[0, 0],
                    device_id=dev(zl=r, c=half, zh=group), device_id_type=MESH,
                ).wait_send()


def per_device(coefficients, exponent, amplitude, centers, momenta, quad_weight):
    vmem, dma = pltpu.VMEM, pltpu.SemaphoreType.DMA
    regular = pltpu.SemaphoreType.REGULAR
    return pl.pallas_call(
        kernel,
        out_shape=pltpu.VMEM((2, 64, 128), F32),
        in_specs=[pl.BlockSpec(memory_space=pl.ANY)] * 6,
        out_specs=pl.BlockSpec(memory_space=pltpu.VMEM),
        scratch_shapes=[
            vmem((4, 4, 2, 64, 1024), BF16), vmem((1, 1024), F32), vmem((1, 1024), F32), vmem((3, 1024), F32),
            vmem((3, 192), F32), vmem((1, 192), F32), vmem((8, 256), F32), vmem((256, 8), F32),
            vmem((384, 1024), BF16),
            vmem((4, 4, 64, 384), F32), vmem((4, 4, 64, 384), BF16), vmem((4, 4, 64, 384), BF16),
            vmem((4, 4, 64, 384), BF16), vmem((4, 3, 64, 384), BF16),
            vmem((3, 64, 384), BF16), vmem((3, 64, 384), BF16), vmem((64, 384), BF16),
            vmem((4, 2, 64, 384), BF16), vmem((4, 2, 64, 384), BF16),
            vmem((4, 4, 128, 128), BF16), vmem((4, 4, 128, 128), F32), vmem((4, 3, 128, 128), BF16),
            vmem((4, 2, 64, 128), BF16), vmem((4, 2, 64, 128), BF16),
            dma((5,)), dma((4,)), regular, regular, regular,
            dma((4,)), dma((4,)), dma((4, 3)), dma((4, 3)), dma((3,)), dma((3,)),
            dma((4,)), dma((4,)), dma((3,)), dma((3,)), dma((3,)), dma((3,)),
            dma((4, 3)), dma((4, 3)), dma((4, 2)), dma((4, 2)),
        ],
        compiler_params=pltpu.CompilerParams(
            collective_id=0, has_side_effects=True, vmem_limit_bytes=60 * 1024 * 1024
        ),
        name="scattering",
    )(
        coefficients.reshape(4, 4, 2, 64, 1024),
        exponent.reshape(1, 1024),
        amplitude.reshape(1, 1024),
        centers,
        momenta,
        quad_weight.reshape(1, 192),
    )


def solution(mesh):
    return jax.shard_map(
        per_device,
        mesh=mesh,
        in_specs=(P(None, "pair"), P("pair"), P("pair"), P(None, "pair"), P(None, "mom"), P("mom")),
        out_specs=P(None, "pair", "mom"),
        check_vma=False,
    )
```

```python
import math

import jax
import jax.numpy as jnp
from jax import lax
from jax.experimental import pallas as pl
from jax.experimental.pallas import tpu as pltpu
from jax.sharding import PartitionSpec as P

MESH = pl.DeviceIdType.MESH
scope = jax.named_scope
BF16, F32 = jnp.bfloat16, jnp.float32
NT = (((1,), (1,)), ((), ()))

RING = (2, 1, 3)
NEAR = (1, 3, 2)
LINE = (2, 1, 3, 0)


def _fit(values, degree):
    import numpy as np

    nodes = 0.125 * (1.0 - np.cos(np.pi * (np.arange(400) + 0.5) / 400))
    weights = np.polynomial.chebyshev.chebfit(8.0 * nodes - 1.0, values(nodes), degree)
    series = np.polynomial.Chebyshev(weights, domain=[0.0, 0.25])
    return [float(c) for c in series.convert(kind=np.polynomial.Polynomial).coef]


def _sin_over(v):
    import numpy as np

    u = np.sqrt(v)
    return 2.0 * np.sin(np.pi * u) / u


def _cos_of(v):
    import numpy as np

    return np.cos(np.pi * np.sqrt(v))


SIN_C = _fit(_sin_over, 4)
COS_C = _fit(_cos_of, 5)


def horner(coefs, v):
    total = coefs[-1] * v + coefs[-2]
    for c in coefs[-3::-1]:
        total = total * v + c
    return total


def encode(x):
    return (x * jnp.abs(x)).astype(BF16)


def decode(y):
    y = y.astype(F32)
    return y * lax.rsqrt(jnp.maximum(jnp.abs(y), 1e-37))


def kernel(
    coef_h, expo_h, amp_h, cen_h, mom_h, qw_h, out,
    coef_v, expo_v, amp_v, cen_v, mom_v, qw_v, rows_v, cols_v, integ,
    prod, core_s, core_r, y_s, y_r, z_s, z_r, r_own, b_all, a_all,
    x_s, x_own, x_r, g_s, g_r,
    in_sem, coef_sem, heard,
    core_ss, core_rs, y_ss, y_rs, z_ss, z_rs, ca_ss, ca_rs, yb_ss, yb_rs, za_ss, za_rs,
    x_ss, x_rs, g_ss, g_rs,
):
    pair, mom = lax.axis_index("pair"), lax.axis_index("mom")
    y, zl, c = pair // 8, (pair // 2) % 4, pair % 2
    x, zh = mom // 4, mom % 4
    z = zh * 4 + zl

    def label(zl):
        return (zl + 3 - 2 * (zh // 2)) % 4

    def holder(group, window):
        return (group + 1 + 2 * (window // 2)) % 4

    group = label(zl)

    def dev(y=y, zl=zl, c=c, x=x, zh=zh):
        return {"pair": y * 8 + zl * 2 + c, "mom": x * 4 + zh}

    def each_way(k, act):
        for step in (2**k, -(2**k)):
            far = z + step

            @pl.when(jnp.logical_and(far >= 0, far < 16))
            def _():
                act(far)

    def ways(k):
        return (z + 16 - 2**k) // 16 + (31 - z - 2**k) // 16

    def tell(k):
        def act(far):
            to = dev(zl=far % 4, zh=far // 4)
            pl.semaphore_signal(heard.at[k], inc=1, device_id=to, device_id_type=MESH)

        each_way(k, act)

    def hear(k):
        pl.semaphore_wait(heard.at[k], ways(k))

    def send(src, dst, ss, rs, to):
        copy = pltpu.make_async_remote_copy(
            src_ref=src, dst_ref=dst, send_sem=ss, recv_sem=rs, device_id=to, device_id_type=MESH
        )
        copy.start()
        return copy

    def bytes_of(ref, ss, rs):
        return pltpu.make_async_remote_copy(
            src_ref=ref, dst_ref=ref, send_sem=ss, recv_sem=rs, device_id=dev(c=1 - c), device_id_type=MESH
        )

    small = [
        pltpu.make_async_copy(h, v, in_sem.at[i])
        for i, (h, v) in enumerate(
            [(expo_h, expo_v), (amp_h, amp_v), (cen_h, cen_v), (mom_h, mom_v), (qw_h, qw_v)]
        )
    ]
    for copy in small:
        copy.start()
    barrier = pltpu.get_barrier_semaphore()
    near = [dev(c=1 - c)]
    near += [dev(y=(y + d) % 4) for d in RING]
    near += [dev(zl=(zl + d) % 4) for d in (1, 2, 3)]
    near += [dev(x=(x + d) % 4) for d in RING]
    for to in near:
        pl.semaphore_signal(barrier, inc=1, device_id=to, device_id_type=MESH)

    def greet(far):
        for core in range(2):
            to = dev(zl=far % 4, zh=far // 4, c=core)
            pl.semaphore_signal(barrier, inc=1, device_id=to, device_id_type=MESH)

    each_way(0, greet)
    greeted = len(near) + 2 * ways(0)

    with scope("small_wait"):
        for copy in small:
            copy.wait()
    coef_in = []
    for t in range(4):
        copy = pltpu.make_async_copy(coef_h.at[:, label((zl + LINE[t]) % 4)], coef_v.at[t], coef_sem.at[t])
        copy.start()
        coef_in.append(copy)
    m = mom_v[...]
    squared = m[0:1] * m[0:1] + m[1:2] * m[1:2] + m[2:3] * m[2:3]
    rows_v[...] = jnp.zeros_like(rows_v)
    rows_v[0:3, 0:192] = m
    rows_v[3:4, 0:192] = squared
    rows_v[4:5, 0:192] = jnp.sqrt(qw_v[...] / (3072.0 * (0.5 * squared + 0.5)))
    cols_v[...] = jnp.transpose(rows_v[...])
    cen_v[...] = cen_v[...] * (0.5 / math.pi)
    expo_v[...] = (-0.25 / math.log(2.0)) / expo_v[...]

    def integrals(i, carry):
        base = pl.multiple_of(i * 16, 16)
        k = cols_v[pl.ds(base, 16), :]
        first = i < 8
        row_c = pl.multiple_of(jnp.where(first, base, base + 128), 16)
        row_s = pl.multiple_of(jnp.where(first, base + 128, base + 192), 16)
        for start in range(0, 1024, 256):
            p = slice(start, start + 256)
            turns = cen_v[0:1, p] * k[:, 0:1] + cen_v[1:2, p] * k[:, 1:2] + cen_v[2:3, p] * k[:, 2:3]
            u = turns - jnp.round(turns)
            v = u * u
            s = horner(SIN_C, v) * u
            envelope = (amp_v[:, p] * jnp.exp2(k[:, 3:4] * expo_v[:, p])) * k[:, 4:5]
            integ[pl.ds(row_c, 16), p] = (envelope - (0.5 * envelope) * (s * s)).astype(BF16)
            integ[pl.ds(row_s, 16), p] = (-((envelope * s) * horner(COS_C, v))).astype(BF16)
        return carry

    with scope("integrals"):
        lax.fori_loop(0, 12, integrals, 0, unroll=12)


    def half(t, core):
        rows = coef_v[t, :, core].reshape(256, 1024)
        return lax.dot_general(rows, integ[...], NT, preferred_element_type=F32).reshape(4, 64, 384)

    def contract(t):
        with scope(f"coef_wait{t}"):
            coef_in[t].wait()
        core_s[t] = encode(half(t, 1 - c))
        if t == 0:
            with scope("barrier"):
                pl.semaphore_wait(barrier, greeted)
        send(core_s.at[t], core_r.at[t], core_ss, core_rs.at[t], dev(c=1 - c))
        prod[t] = half(t, c)

    def spread(t):
        with scope(f"core_wait{t}"):
            bytes_of(core_r.at[t], core_ss, core_rs.at[t]).wait_recv()
        total = prod[t] + decode(core_r[t])
        prod[t] = total
        y_s[t] = encode(total)
        for i, d in enumerate(RING):
            send(y_s.at[t, (y + d) % 4], y_r.at[t, i], y_ss, y_rs.at[t], dev(y=(y + d) % 4))

    contract(0)
    contract(1)
    for t in range(4):
        spread(t)
        if t < 2:
            contract(t + 2)
        if t == 1:
            tell(0)

    for t in range(4):
        with scope(f"y_wait{t}"):
            bytes_of(y_r.at[t], y_ss, y_rs.at[t]).wait_recv()
        total = prod[t, y]
        for i in range(3):
            total = total + decode(y_r[t, i])
        if t < 3:
            z_s[t] = encode(total)
            send(z_s.at[t], z_r.at[t], z_ss, z_rs, dev(zl=(zl + LINE[t]) % 4))
        if t in (0, 2):
            hear(t // 2)
            tell(t // 2 + 1)
    with scope("z_wait"):
        bytes_of(z_r, z_ss, z_rs).wait_recv()
    for t in range(3):
        total = total + decode(z_r[t])
    r_own[...] = (total * 65536.0).astype(BF16)

    ca = [send(r_own, a_all.at[group, c], ca_ss, ca_rs.at[0], dev(c=1 - c))]
    yb = [
        send(r_own, b_all.at[y, 0], yb_ss, yb_rs.at[i], dev(y=(y + d) % 4)) for i, d in enumerate(NEAR)
    ]
    za = [
        send(r_own, a_all.at[group, c], za_ss, za_rs.at[i], dev(zl=(zl + d) % 4)) for i, d in enumerate(NEAR)
    ]
    lane = lax.broadcasted_iota(jnp.int32, (64, 128), 1)

    def turn(n):
        rows = b_all[n, 0].astype(F32)
        last = pltpu.roll(rows[:, 256:384], 64, 1) * jnp.where(lane < 64, 1.0, -1.0)
        b_all[n, 1] = jnp.concatenate([rows[:, 128:256], -rows[:, 0:128], last], axis=1).astype(BF16)

    b_all[y, 0] = r_own[...]
    a_all[group, c] = r_own[...]
    hear(2)
    tell(3)
    x_c = []
    with scope("ca_wait0"):
        ca[0].wait_recv()
    left = a_all[group].reshape(128, 384)
    def forward(i):
        with scope(f"za_wait{i}"):
            za[i].wait_recv()
        here = a_all.at[label((zl + 4 - NEAR[i]) % 4), c]
        ca.append(send(here, here, ca_ss, ca_rs.at[i + 1], dev(c=1 - c)))

    for i, d in enumerate((0, *NEAR)):
        n = (y + 4 - d) % 4
        if d:
            with scope(f"yb_wait{i}"):
                yb[i - 1].wait_recv()
        turn(n)
        block = lax.dot_general(left, b_all[n].reshape(128, 384), NT, preferred_element_type=F32)
        x_own[0, n] = block.reshape(2, 64, 128)
        x_s[0, n] = encode(block).reshape(2, 64, 128)
        e = (n - x + 4) % 4

        @pl.when(e > 0)
        def _():
            send(x_s.at[0, n], x_r.at[0, e - 1], x_ss, x_rs.at[0], dev(x=n))

        if d:
            forward(i - 1)

    halves = [(i, half) for half in range(2) for i in range(1, 4)]
    for i, half in halves:
        core = (c + half) % 2
        if half:
            with scope(f"ca_wait{i}"):
                ca[i].wait_recv()
        left = a_all[label((zl + 4 - (0, *NEAR)[i]) % 4), core]
        block = lax.dot_general(left, b_all[...].reshape(512, 384), NT, preferred_element_type=F32)
        for n in range(4):
            x_own[i, n, core] = block[:, n * 128 : n * 128 + 128]
            x_s[i, n, core] = encode(block[:, n * 128 : n * 128 + 128])
        for j, e in enumerate(RING):
            n = (x + e) % 4
            send(x_s.at[i, n, core], x_r.at[i, j, core], x_ss, x_rs.at[i + 3 * half], dev(x=n))

    with scope("hear3"):
        hear(3)
    for k, (i, half) in enumerate([(0, 0), (0, 1), *halves]):
        r = label((zl + 4 - (0, *NEAR)[i]) % 4)
        core = (c + half) % 2
        if k != 1:
            with scope(f"x_wait{i}{half}"):
                landed = x_r.at[i, :, core] if i else x_r.at[0]
                bytes_of(landed, x_ss, x_rs.at[i + 3 * half]).wait_recv()
        total = x_own[i, x, core]
        for j in range(3):
            total = total + decode(x_r[i, j, core])
        g_s[i, core] = encode(total)
        to = (g_s.at[i, core], g_r.at[zh, c], g_ss.at[half], g_rs.at[zh], dev(zl=r, c=core, zh=group))
        if half:
            send(*to)
        else:
            here = jnp.logical_and(r == zl, zh == group)

            @pl.when(here)
            def _():
                g_r[zh, c] = g_s[i, core]

            @pl.when(jnp.logical_not(here))
            def _():
                send(*to)

    with scope("left"):
        for ref, sem in (
            (core_r, core_ss), (y_r, y_ss), (z_r, z_ss), (a_all.at[:, 0], ca_ss), (z_r, yb_ss), (z_r, za_ss), (x_r, x_ss)
        ):
            bytes_of(ref, sem, z_rs).wait_send()

    total = [jnp.zeros((64, 128), F32)] * 2
    for a in range(4):
        here = jnp.logical_and(holder(zh, a) == zl, zh == a)

        @pl.when(here)
        def _():
            bytes_of(g_r.at[a, 0], g_ss.at[0], g_rs.at[a]).wait_recv()

        @pl.when(jnp.logical_not(here))
        def _():
            with scope(f"g_wait{a}"):
                bytes_of(g_r.at[a], g_ss.at[0], g_rs.at[a]).wait_recv()

        for core in range(2):
            total[core] = total[core] + decode(g_r[a, core])
    first, second = total[0] * 2.0**-32, total[1] * 2.0**-32
    out[0] = jnp.where(lane < 64, first, pltpu.roll(second, 64, 1))
    out[1] = jnp.where(lane < 64, pltpu.roll(first, 64, 1), second)

    bytes_of(g_s.at[:, 0], g_ss.at[1], z_rs).wait_send()
    here = group == zh

    @pl.when(here)
    def _():
        bytes_of(g_s.at[0:3, 0], g_ss.at[0], z_rs).wait_send()

    @pl.when(jnp.logical_not(here))
    def _():
        bytes_of(g_s.at[:, 0], g_ss.at[0], z_rs).wait_send()


def per_device(coefficients, exponent, amplitude, centers, momenta, quad_weight):
    vmem, dma = pltpu.VMEM, pltpu.SemaphoreType.DMA
    return pl.pallas_call(
        kernel,
        out_shape=pltpu.VMEM((2, 64, 128), F32),
        in_specs=[pl.BlockSpec(memory_space=pl.ANY)] * 6,
        out_specs=pl.BlockSpec(memory_space=pltpu.VMEM),
        scratch_shapes=[
            vmem((4, 4, 2, 64, 1024), BF16), vmem((1, 1024), F32), vmem((1, 1024), F32), vmem((3, 1024), F32),
            vmem((3, 192), F32), vmem((1, 192), F32), vmem((8, 256), F32), vmem((256, 8), F32),
            vmem((384, 1024), BF16),
            vmem((4, 4, 64, 384), F32), vmem((4, 4, 64, 384), BF16), vmem((4, 4, 64, 384), BF16),
            vmem((4, 4, 64, 384), BF16), vmem((4, 3, 64, 384), BF16),
            vmem((3, 64, 384), BF16), vmem((3, 64, 384), BF16), vmem((64, 384), BF16),
            vmem((4, 2, 64, 384), BF16), vmem((4, 2, 64, 384), BF16),
            vmem((4, 4, 2, 64, 128), BF16), vmem((4, 4, 2, 64, 128), F32), vmem((4, 3, 2, 64, 128), BF16),
            vmem((4, 2, 64, 128), BF16), vmem((4, 2, 64, 128), BF16),
            dma((5,)), dma((4,)), pltpu.SemaphoreType.REGULAR((4,)),
            dma, dma((4,)), dma, dma((4,)), dma, dma, dma, dma((4,)), dma, dma((3,)), dma, dma((3,)),
            dma, dma((7,)), dma((2,)), dma((4,)),
        ],
        compiler_params=pltpu.CompilerParams(
            collective_id=0, has_side_effects=True, vmem_limit_bytes=60 * 1024 * 1024
        ),
        name="scattering",
    )(
        coefficients.reshape(4, 4, 2, 64, 1024),
        exponent.reshape(1, 1024),
        amplitude.reshape(1, 1024),
        centers,
        momenta,
        quad_weight.reshape(1, 192),
    )


def solution(mesh):
    return jax.shard_map(
        per_device,
        mesh=mesh,
        in_specs=(P(None, "pair"), P("pair"), P("pair"), P(None, "pair"), P(None, "mom"), P("mom")),
        out_specs=P(None, "pair", "mom"),
        check_vma=False,
    )
```

```python
import math

import jax
import jax.numpy as jnp
from jax import lax
from jax.experimental import pallas as pl
from jax.experimental.pallas import tpu as pltpu
from jax.sharding import PartitionSpec as P

MESH = pl.DeviceIdType.MESH
scope = jax.named_scope
BF16, F32 = jnp.bfloat16, jnp.float32
NT = (((1,), (1,)), ((), ()))

RING = (2, 1, 3)
NEAR = (1, 3, 2)
ALONG = (3, 2, 1)
LINE = (2, 1, 3, 0)


def _fit(values, degree):
    import numpy as np

    nodes = 0.125 * (1.0 - np.cos(np.pi * (np.arange(400) + 0.5) / 400))
    weights = np.polynomial.chebyshev.chebfit(8.0 * nodes - 1.0, values(nodes), degree)
    series = np.polynomial.Chebyshev(weights, domain=[0.0, 0.25])
    return [float(c) for c in series.convert(kind=np.polynomial.Polynomial).coef]


def _sin_over(v):
    import numpy as np

    u = np.sqrt(v)
    return 2.0 * np.sin(np.pi * u) / u


def _cos_of(v):
    import numpy as np

    return np.cos(np.pi * np.sqrt(v))


SIN_C = _fit(_sin_over, 4)
COS_C = _fit(_cos_of, 5)


def horner(coefs, v):
    total = coefs[-1] * v + coefs[-2]
    for c in coefs[-3::-1]:
        total = total * v + c
    return total


def encode(x):
    return (x * jnp.abs(x)).astype(BF16)


def decode(y):
    y = y.astype(F32)
    return y * lax.rsqrt(jnp.maximum(jnp.abs(y), 1e-37))


def kernel(
    coef_h, expo_h, amp_h, cen_h, mom_h, qw_h, out,
    coef_v, expo_v, amp_v, cen_v, mom_v, qw_v, rows_v, cols_v, integ,
    prod, core_s, core_r, y_s, y_r, z_s, z_r, r_own, b_all, a_all,
    x_s, x_own, x_r, g_s, g_r,
    in_sem, coef_sem, heard,
    core_ss, core_rs, y_ss, y_rs, z_ss, z_rs, ca_ss, ca_rs, yb_ss, yb_rs, za_ss, za_rs,
    x_ss, x_rs, g_ss, g_rs,
):
    pair, mom = lax.axis_index("pair"), lax.axis_index("mom")
    y, zl, c = pair // 8, (pair // 2) % 4, pair % 2
    x, zh = mom // 4, mom % 4
    z = zh * 4 + zl

    def label(zl):
        return (zl + 3 - 2 * (zh // 2)) % 4

    def holder(group, window):
        return (group + 1 + 2 * (window // 2)) % 4

    group = label(zl)

    def dev(y=y, zl=zl, c=c, x=x, zh=zh):
        return {"pair": y * 8 + zl * 2 + c, "mom": x * 4 + zh}

    def each_way(k, act):
        for step in (2**k, -(2**k)):
            far = z + step

            @pl.when(jnp.logical_and(far >= 0, far < 16))
            def _():
                act(far)

    def ways(k):
        return (z + 16 - 2**k) // 16 + (31 - z - 2**k) // 16

    def tell(k):
        def act(far):
            to = dev(zl=far % 4, zh=far // 4)
            pl.semaphore_signal(heard.at[k], inc=1, device_id=to, device_id_type=MESH)

        each_way(k, act)

    def hear(k):
        pl.semaphore_wait(heard.at[k], ways(k))

    def send(src, dst, ss, rs, to):
        copy = pltpu.make_async_remote_copy(
            src_ref=src, dst_ref=dst, send_sem=ss, recv_sem=rs, device_id=to, device_id_type=MESH
        )
        copy.start()
        return copy

    def bytes_of(ref, ss, rs):
        return pltpu.make_async_remote_copy(
            src_ref=ref, dst_ref=ref, send_sem=ss, recv_sem=rs, device_id=dev(c=1 - c), device_id_type=MESH
        )

    small = [
        pltpu.make_async_copy(h, v, in_sem.at[i])
        for i, (h, v) in enumerate(
            [(expo_h, expo_v), (amp_h, amp_v), (cen_h, cen_v), (mom_h, mom_v), (qw_h, qw_v)]
        )
    ]
    for copy in small:
        copy.start()
    barrier = pltpu.get_barrier_semaphore()
    near = [dev(c=1 - c)]
    near += [dev(y=(y + d) % 4) for d in RING]
    near += [dev(zl=(zl + d) % 4) for d in (1, 2, 3)]
    near += [dev(x=(x + d) % 4) for d in RING]
    for to in near:
        pl.semaphore_signal(barrier, inc=1, device_id=to, device_id_type=MESH)

    def greet(far):
        for core in range(2):
            to = dev(zl=far % 4, zh=far // 4, c=core)
            pl.semaphore_signal(barrier, inc=1, device_id=to, device_id_type=MESH)

    each_way(0, greet)
    greeted = len(near) + 2 * ways(0)

    with scope("small_wait"):
        for copy in small:
            copy.wait()
    coef_in = []
    for t in range(4):
        copy = pltpu.make_async_copy(coef_h.at[:, label((zl + LINE[t]) % 4)], coef_v.at[t], coef_sem.at[t])
        copy.start()
        coef_in.append(copy)
    m = mom_v[...]
    squared = m[0:1] * m[0:1] + m[1:2] * m[1:2] + m[2:3] * m[2:3]
    rows_v[...] = jnp.zeros_like(rows_v)
    rows_v[0:3, 0:192] = m
    rows_v[3:4, 0:192] = squared
    rows_v[4:5, 0:192] = jnp.sqrt(qw_v[...] / (3072.0 * (0.5 * squared + 0.5)))
    cols_v[...] = jnp.transpose(rows_v[...])
    cen_v[...] = cen_v[...] * (0.5 / math.pi)
    expo_v[...] = (-0.25 / math.log(2.0)) / expo_v[...]

    def integrals(i, carry):
        base = pl.multiple_of(i * 16, 16)
        k = cols_v[pl.ds(base, 16), :]
        first = i < 8
        row_c = pl.multiple_of(jnp.where(first, base, base + 128), 16)
        row_s = pl.multiple_of(jnp.where(first, base + 128, base + 192), 16)
        for start in range(0, 1024, 256):
            p = slice(start, start + 256)
            turns = cen_v[0:1, p] * k[:, 0:1] + cen_v[1:2, p] * k[:, 1:2] + cen_v[2:3, p] * k[:, 2:3]
            u = turns - jnp.round(turns)
            v = u * u
            s = horner(SIN_C, v) * u
            envelope = (amp_v[:, p] * jnp.exp2(k[:, 3:4] * expo_v[:, p])) * k[:, 4:5]
            integ[pl.ds(row_c, 16), p] = (envelope - (0.5 * envelope) * (s * s)).astype(BF16)
            integ[pl.ds(row_s, 16), p] = (-((envelope * s) * horner(COS_C, v))).astype(BF16)
        return carry

    with scope("integrals"):
        lax.fori_loop(0, 12, integrals, 0, unroll=12)


    def half(t, core):
        rows = coef_v[t, :, core].reshape(256, 1024)
        return lax.dot_general(rows, integ[...], NT, preferred_element_type=F32).reshape(4, 64, 384)

    def contract(t):
        with scope(f"coef_wait{t}"):
            coef_in[t].wait()
        core_s[t] = encode(half(t, 1 - c))
        if t == 0:
            with scope("barrier"):
                pl.semaphore_wait(barrier, greeted)
            tell(0)
        send(core_s.at[t], core_r.at[t], core_ss, core_rs.at[t], dev(c=1 - c))
        prod[t] = half(t, c)

    def spread(t):
        with scope(f"core_wait{t}"):
            bytes_of(core_r.at[t], core_ss, core_rs.at[t]).wait_recv()
        total = prod[t] + decode(core_r[t])
        prod[t] = total
        y_s[t] = encode(total)
        for i, d in enumerate(RING):
            send(y_s.at[t, (y + d) % 4], y_r.at[t, i], y_ss, y_rs.at[t], dev(y=(y + d) % 4))

    contract(0)
    contract(1)
    for t in range(4):
        spread(t)
        if t < 2:
            contract(t + 2)
        if t == 1:
            hear(0)
            tell(1)
        if t == 3:
            hear(1)
            tell(2)

    for t in range(4):
        with scope(f"y_wait{t}"):
            bytes_of(y_r.at[t], y_ss, y_rs.at[t]).wait_recv()
        total = prod[t, y]
        for i in range(3):
            total = total + decode(y_r[t, i])
        if t < 3:
            z_s[t] = encode(total)
            send(z_s.at[t], z_r.at[t], z_ss, z_rs, dev(zl=(zl + LINE[t]) % 4))
        if t == 2:
            hear(2)
            tell(3)
    with scope("z_wait"):
        bytes_of(z_r, z_ss, z_rs).wait_recv()
    for t in range(3):
        total = total + decode(z_r[t])
    r_own[...] = (total * 65536.0).astype(BF16)

    ca = [send(r_own, a_all.at[group, c], ca_ss, ca_rs.at[0], dev(c=1 - c))]
    yb = [
        send(r_own, b_all.at[y, 0], yb_ss, yb_rs.at[i], dev(y=(y + d) % 4)) for i, d in enumerate(NEAR)
    ]
    za = [
        send(r_own, a_all.at[group, c], za_ss, za_rs.at[i], dev(zl=(zl + d) % 4)) for i, d in enumerate(ALONG)
    ]
    lane = lax.broadcasted_iota(jnp.int32, (64, 128), 1)

    def turn(n):
        rows = b_all[n, 0].astype(F32)
        last = pltpu.roll(rows[:, 256:384], 64, 1) * jnp.where(lane < 64, 1.0, -1.0)
        b_all[n, 1] = jnp.concatenate([rows[:, 128:256], -rows[:, 0:128], last], axis=1).astype(BF16)

    b_all[y, 0] = r_own[...]
    a_all[group, c] = r_own[...]
    x_c = []
    with scope("ca_wait0"):
        ca[0].wait_recv()
    left = a_all[group].reshape(128, 384)
    def forward(i):
        with scope(f"za_wait{i}"):
            za[i].wait_recv()
        here = a_all.at[label((zl + 4 - ALONG[i]) % 4), c]
        ca.append(send(here, here, ca_ss, ca_rs.at[i + 1], dev(c=1 - c)))

    for i, d in enumerate((0, *NEAR)):
        n = (y + 4 - d) % 4
        if d:
            with scope(f"yb_wait{i}"):
                yb[i - 1].wait_recv()
        turn(n)
        block = lax.dot_general(left, b_all[n].reshape(128, 384), NT, preferred_element_type=F32)
        x_own[0, n] = block.reshape(2, 64, 128)
        x_s[0, n] = encode(block).reshape(2, 64, 128)
        e = (n - x + 4) % 4

        @pl.when(e > 0)
        def _():
            send(x_s.at[0, n], x_r.at[0, e - 1], x_ss, x_rs.at[0], dev(x=n))

        if d:
            forward(i - 1)

    halves = [(i, half) for half in range(2) for i in range(1, 4)]
    for i, half in halves:
        core = (c + half) % 2
        if half:
            with scope(f"ca_wait{i}"):
                ca[i].wait_recv()
        left = a_all[label((zl + 4 - (0, *ALONG)[i]) % 4), core]
        block = lax.dot_general(left, b_all[...].reshape(512, 384), NT, preferred_element_type=F32)
        for n in range(4):
            x_own[i, n, core] = block[:, n * 128 : n * 128 + 128]
            x_s[i, n, core] = encode(block[:, n * 128 : n * 128 + 128])
        for j, e in enumerate(RING):
            n = (x + e) % 4
            send(x_s.at[i, n, core], x_r.at[i, j, core], x_ss, x_rs.at[i + 3 * half], dev(x=n))

    with scope("hear3"):
        hear(3)
    for k, (i, half) in enumerate([(0, 0), (0, 1), *halves]):
        r = label((zl + 4 - (0, *ALONG)[i]) % 4)
        core = (c + half) % 2
        if k != 1:
            with scope(f"x_wait{i}{half}"):
                landed = x_r.at[i, :, core] if i else x_r.at[0]
                bytes_of(landed, x_ss, x_rs.at[i + 3 * half]).wait_recv()
        total = x_own[i, x, core]
        for j in range(3):
            total = total + decode(x_r[i, j, core])
        g_s[i, core] = encode(total)
        to = (g_s.at[i, core], g_r.at[zh, c], g_ss.at[half], g_rs.at[zh], dev(zl=r, c=core, zh=group))
        if half:
            send(*to)
        else:
            here = jnp.logical_and(r == zl, zh == group)

            @pl.when(here)
            def _():
                g_r[zh, c] = g_s[i, core]

            @pl.when(jnp.logical_not(here))
            def _():
                send(*to)

    with scope("left"):
        for ref, sem in (
            (core_r, core_ss), (y_r, y_ss), (z_r, z_ss), (a_all.at[:, 0], ca_ss), (z_r, yb_ss), (z_r, za_ss), (x_r, x_ss)
        ):
            bytes_of(ref, sem, z_rs).wait_send()

    total = [jnp.zeros((64, 128), F32)] * 2
    for a in range(4):
        here = jnp.logical_and(holder(zh, a) == zl, zh == a)

        @pl.when(here)
        def _():
            bytes_of(g_r.at[a, 0], g_ss.at[0], g_rs.at[a]).wait_recv()

        @pl.when(jnp.logical_not(here))
        def _():
            with scope(f"g_wait{a}"):
                bytes_of(g_r.at[a], g_ss.at[0], g_rs.at[a]).wait_recv()

        for core in range(2):
            total[core] = total[core] + decode(g_r[a, core])
    first, second = total[0] * 2.0**-32, total[1] * 2.0**-32
    out[0] = jnp.where(lane < 64, first, pltpu.roll(second, 64, 1))
    out[1] = jnp.where(lane < 64, pltpu.roll(first, 64, 1), second)

    bytes_of(g_s.at[:, 0], g_ss.at[1], z_rs).wait_send()
    here = group == zh

    @pl.when(here)
    def _():
        bytes_of(g_s.at[0:3, 0], g_ss.at[0], z_rs).wait_send()

    @pl.when(jnp.logical_not(here))
    def _():
        bytes_of(g_s.at[:, 0], g_ss.at[0], z_rs).wait_send()


def per_device(coefficients, exponent, amplitude, centers, momenta, quad_weight):
    vmem, dma = pltpu.VMEM, pltpu.SemaphoreType.DMA
    return pl.pallas_call(
        kernel,
        out_shape=pltpu.VMEM((2, 64, 128), F32),
        in_specs=[pl.BlockSpec(memory_space=pl.ANY)] * 6,
        out_specs=pl.BlockSpec(memory_space=pltpu.VMEM),
        scratch_shapes=[
            vmem((4, 4, 2, 64, 1024), BF16), vmem((1, 1024), F32), vmem((1, 1024), F32), vmem((3, 1024), F32),
            vmem((3, 192), F32), vmem((1, 192), F32), vmem((8, 256), F32), vmem((256, 8), F32),
            vmem((384, 1024), BF16),
            vmem((4, 4, 64, 384), F32), vmem((4, 4, 64, 384), BF16), vmem((4, 4, 64, 384), BF16),
            vmem((4, 4, 64, 384), BF16), vmem((4, 3, 64, 384), BF16),
            vmem((3, 64, 384), BF16), vmem((3, 64, 384), BF16), vmem((64, 384), BF16),
            vmem((4, 2, 64, 384), BF16), vmem((4, 2, 64, 384), BF16),
            vmem((4, 4, 2, 64, 128), BF16), vmem((4, 4, 2, 64, 128), F32), vmem((4, 3, 2, 64, 128), BF16),
            vmem((4, 2, 64, 128), BF16), vmem((4, 2, 64, 128), BF16),
            dma((5,)), dma((4,)), pltpu.SemaphoreType.REGULAR((4,)),
            dma, dma((4,)), dma, dma((4,)), dma, dma, dma, dma((4,)), dma, dma((3,)), dma, dma((3,)),
            dma, dma((7,)), dma((2,)), dma((4,)),
        ],
        compiler_params=pltpu.CompilerParams(
            collective_id=0, has_side_effects=True, vmem_limit_bytes=60 * 1024 * 1024
        ),
        name="scattering",
    )(
        coefficients.reshape(4, 4, 2, 64, 1024),
        exponent.reshape(1, 1024),
        amplitude.reshape(1, 1024),
        centers,
        momenta,
        quad_weight.reshape(1, 192),
    )


def solution(mesh):
    return jax.shard_map(
        per_device,
        mesh=mesh,
        in_specs=(P(None, "pair"), P("pair"), P("pair"), P(None, "pair"), P(None, "mom"), P("mom")),
        out_specs=P(None, "pair", "mom"),
        check_vma=False,
    )
```

```python
import math

import jax
import jax.numpy as jnp
from jax import lax
from jax.experimental import pallas as pl
from jax.experimental.pallas import tpu as pltpu
from jax.sharding import PartitionSpec as P

MESH = pl.DeviceIdType.MESH
scope = jax.named_scope
BF16, F32 = jnp.bfloat16, jnp.float32
NT = (((1,), (1,)), ((), ()))

RING = (2, 1, 3)
NEAR = (1, 3, 2)
ALL, LOW, HIGH = pl.ds(0, 64), pl.ds(0, 32), pl.ds(32, 32)
PARTS = ((ALL,), (ALL,), (LOW, HIGH), (ALL,))
ALONG = (3, 2, 1)
LINE = (2, 1, 3, 0)


def _fit(values, degree):
    import numpy as np

    nodes = 0.125 * (1.0 - np.cos(np.pi * (np.arange(400) + 0.5) / 400))
    weights = np.polynomial.chebyshev.chebfit(8.0 * nodes - 1.0, values(nodes), degree)
    series = np.polynomial.Chebyshev(weights, domain=[0.0, 0.25])
    return [float(c) for c in series.convert(kind=np.polynomial.Polynomial).coef]


def _sin_over(v):
    import numpy as np

    u = np.sqrt(v)
    return math.sqrt(2.0) * np.sin(np.pi * u) / u


def _cos_of(v):
    import numpy as np

    return -math.sqrt(2.0) * np.cos(np.pi * np.sqrt(v))


SIN_C = _fit(_sin_over, 4)
COS_C = _fit(_cos_of, 4)


def horner(coefs, v):
    total = coefs[-1] * v + coefs[-2]
    for c in coefs[-3::-1]:
        total = total * v + c
    return total


def encode(x):
    return (x * jnp.abs(x)).astype(BF16)


def decode(y):
    y = y.astype(F32)
    return y * lax.rsqrt(jnp.maximum(jnp.abs(y), 1e-37))


def kernel(
    coef_h, expo_h, amp_h, cen_h, mom_h, qw_h, out,
    coef_v, expo_v, amp_v, cen_v, mom_v, qw_v, rows_v, cols_v, integ,
    prod, core_s, core_r, y_s, y_r, z_s, z_r, r_own, b_all, a_all,
    x_s, x_own, x_r, g_s, g_r,
    in_sem, coef_sem, heard,
    core_ss, core_rs, y_ss, y_rs, z_ss, z_rs, ca_ss, ca_rs, yb_ss, yb_rs, za_ss, za_rs,
    x_ss, x_rs, g_ss, g_rs,
):
    pair, mom = lax.axis_index("pair"), lax.axis_index("mom")
    y, zl, c = pair // 8, (pair // 2) % 4, pair % 2
    x, zh = mom // 4, mom % 4
    z = zh * 4 + zl

    def label(zl):
        return (zl + 3 - 2 * (zh // 2)) % 4

    def holder(group, window):
        return (group + 1 + 2 * (window // 2)) % 4

    group = label(zl)

    def dev(y=y, zl=zl, c=c, x=x, zh=zh):
        return {"pair": y * 8 + zl * 2 + c, "mom": x * 4 + zh}

    def each_way(k, act):
        for step in (2**k, -(2**k)):
            far = z + step

            @pl.when(jnp.logical_and(far >= 0, far < 16))
            def _():
                act(far)

    def ways(k):
        return (z + 16 - 2**k) // 16 + (31 - z - 2**k) // 16

    def tell(k):
        def act(far):
            to = dev(zl=far % 4, zh=far // 4)
            pl.semaphore_signal(heard.at[k], inc=1, device_id=to, device_id_type=MESH)

        each_way(k, act)

    def hear(k):
        pl.semaphore_wait(heard.at[k], ways(k))

    def send(src, dst, ss, rs, to):
        copy = pltpu.make_async_remote_copy(
            src_ref=src, dst_ref=dst, send_sem=ss, recv_sem=rs, device_id=to, device_id_type=MESH
        )
        copy.start()
        return copy

    def bytes_of(ref, ss, rs):
        return pltpu.make_async_remote_copy(
            src_ref=ref, dst_ref=ref, send_sem=ss, recv_sem=rs, device_id=dev(c=1 - c), device_id_type=MESH
        )

    small = [
        pltpu.make_async_copy(h, v, in_sem.at[i])
        for i, (h, v) in enumerate(
            [(expo_h, expo_v), (amp_h, amp_v), (cen_h, cen_v), (mom_h, mom_v), (qw_h, qw_v)]
        )
    ]
    for copy in small:
        copy.start()
    barrier = pltpu.get_barrier_semaphore()
    near = [dev(c=1 - c)]
    near += [dev(y=(y + d) % 4) for d in RING]
    near += [dev(zl=(zl + d) % 4) for d in (1, 2, 3)]
    near += [dev(x=(x + d) % 4) for d in RING]
    for to in near:
        pl.semaphore_signal(barrier, inc=1, device_id=to, device_id_type=MESH)

    def greet(far):
        for core in range(2):
            to = dev(zl=far % 4, zh=far // 4, c=core)
            pl.semaphore_signal(barrier, inc=1, device_id=to, device_id_type=MESH)

    each_way(0, greet)
    greeted = len(near) + 2 * ways(0)

    with scope("small_wait"):
        for copy in small:
            copy.wait()
    coef_in = []
    for t in range(4):
        copy = pltpu.make_async_copy(coef_h.at[:, label((zl + LINE[t]) % 4)], coef_v.at[t], coef_sem.at[t])
        copy.start()
        coef_in.append(copy)
    m = mom_v[...]
    squared = m[0:1] * m[0:1] + m[1:2] * m[1:2] + m[2:3] * m[2:3]
    rows_v[...] = jnp.zeros_like(rows_v)
    rows_v[0:3, 0:192] = m
    rows_v[3:4, 0:192] = squared
    rows_v[4:5, 0:192] = jnp.sqrt(qw_v[...] / (3072.0 * (0.5 * squared + 0.5)))
    cols_v[...] = jnp.transpose(rows_v[...])
    cen_v[...] = cen_v[...] * (0.5 / math.pi)
    expo_v[...] = (-0.25 / math.log(2.0)) / expo_v[...]

    def integrals(i, carry):
        base = pl.multiple_of(i * 16, 16)
        k = cols_v[pl.ds(base, 16), :]
        first = i < 8
        row_c = pl.multiple_of(jnp.where(first, base, base + 128), 16)
        row_s = pl.multiple_of(jnp.where(first, base + 128, base + 192), 16)
        for start in range(0, 1024, 256):
            p = slice(start, start + 256)
            turns = cen_v[0:1, p] * k[:, 0:1] + cen_v[1:2, p] * k[:, 1:2] + cen_v[2:3, p] * k[:, 2:3]
            u = turns - jnp.round(turns)
            v = u * u
            s = horner(SIN_C, v) * u
            envelope = (amp_v[:, p] * jnp.exp2(k[:, 3:4] * expo_v[:, p])) * k[:, 4:5]
            product = envelope * s
            integ[pl.ds(row_c, 16), p] = (envelope - product * s).astype(BF16)
            integ[pl.ds(row_s, 16), p] = (product * horner(COS_C, v)).astype(BF16)
        return carry

    with scope("integrals"):
        lax.fori_loop(0, 12, integrals, 0, unroll=12)


    def half(t, core):
        rows = coef_v[t, :, core].reshape(256, 1024)
        return lax.dot_general(rows, integ[...], NT, preferred_element_type=F32).reshape(4, 64, 384)

    def contract(t):
        with scope(f"coef_wait{t}"):
            coef_in[t].wait()
        core_s[t] = encode(half(t, 1 - c))
        if t == 0:
            with scope("barrier"):
                pl.semaphore_wait(barrier, greeted)
            tell(0)
        send(core_s.at[t], core_r.at[t], core_ss, core_rs.at[t], dev(c=1 - c))
        prod[t] = half(t, c)

    def spread(t):
        with scope(f"core_wait{t}"):
            bytes_of(core_r.at[t], core_ss, core_rs.at[t]).wait_recv()
        total = prod[t] + decode(core_r[t])
        prod[t] = total
        y_s[t] = encode(total)
        for k, rows in enumerate(PARTS[t]):
            for i, d in enumerate(RING):
                to = dev(y=(y + d) % 4)
                send(y_s.at[t, (y + d) % 4, rows], y_r.at[t, i, rows], y_ss, y_rs.at[t + 4 * k], to)

    contract(0)
    contract(1)
    for t in range(4):
        spread(t)
        if t < 2:
            contract(t + 2)
        if t == 1:
            hear(0)
            tell(1)
        if t == 3:
            hear(1)
            tell(2)

    for t in range(4):
        for k, rows in enumerate(PARTS[t]):
            with scope(f"y_wait{t}{k}"):
                bytes_of(y_r.at[t, :, rows], y_ss, y_rs.at[t + 4 * k]).wait_recv()
            total = prod[t, y, rows]
            for i in range(3):
                total = total + decode(y_r[t, i, rows])
            if t < 3:
                z_s[t, rows] = encode(total)
                send(z_s.at[t, rows], z_r.at[t, rows], z_ss, z_rs, dev(zl=(zl + LINE[t]) % 4))
        if t == 2:
            hear(2)
            tell(3)

    with scope("z_wait"):
        bytes_of(z_r, z_ss, z_rs).wait_recv()
    for t in range(3):
        total = total + decode(z_r[t])
    r_own[...] = (total * 65536.0).astype(BF16)

    ca = [send(r_own, a_all.at[group, c], ca_ss, ca_rs.at[0], dev(c=1 - c))]
    yb = [
        send(r_own, b_all.at[y, 0], yb_ss, yb_rs.at[i], dev(y=(y + d) % 4)) for i, d in enumerate(NEAR)
    ]
    za = [
        send(r_own, a_all.at[group, c], za_ss, za_rs.at[i], dev(zl=(zl + d) % 4)) for i, d in enumerate(ALONG)
    ]
    lane = lax.broadcasted_iota(jnp.int32, (64, 128), 1)

    def turn(n):
        rows = b_all[n, 0].astype(F32)
        last = pltpu.roll(rows[:, 256:384], 64, 1) * jnp.where(lane < 64, 1.0, -1.0)
        b_all[n, 1] = jnp.concatenate([rows[:, 128:256], -rows[:, 0:128], last], axis=1).astype(BF16)

    b_all[y, 0] = r_own[...]
    a_all[group, c] = r_own[...]
    x_c = []
    with scope("ca_wait0"):
        ca[0].wait_recv()
    left = a_all[group].reshape(128, 384)
    def forward(i):
        with scope(f"za_wait{i}"):
            za[i].wait_recv()
        here = a_all.at[label((zl + 4 - ALONG[i]) % 4), c]
        ca.append(send(here, here, ca_ss, ca_rs.at[i + 1], dev(c=1 - c)))

    for i, d in enumerate((0, *NEAR)):
        n = (y + 4 - d) % 4
        if d:
            with scope(f"yb_wait{i}"):
                yb[i - 1].wait_recv()
        turn(n)
        block = lax.dot_general(left, b_all[n].reshape(128, 384), NT, preferred_element_type=F32)
        x_own[0, n] = block.reshape(2, 64, 128)
        x_s[0, n] = encode(block).reshape(2, 64, 128)
        e = (n - x + 4) % 4

        @pl.when(e > 0)
        def _():
            send(x_s.at[0, n], x_r.at[0, e - 1], x_ss, x_rs.at[0], dev(x=n))

        if d:
            forward(i - 1)

    halves = [(i, half) for half in range(2) for i in range(1, 4)]
    for i, half in halves:
        core = (c + half) % 2
        if half:
            with scope(f"ca_wait{i}"):
                ca[i].wait_recv()
        left = a_all[label((zl + 4 - (0, *ALONG)[i]) % 4), core]
        block = lax.dot_general(left, b_all[...].reshape(512, 384), NT, preferred_element_type=F32)
        for n in range(4):
            x_own[i, n, core] = block[:, n * 128 : n * 128 + 128]
            x_s[i, n, core] = encode(block[:, n * 128 : n * 128 + 128])
        for j, e in enumerate(RING):
            n = (x + e) % 4
            send(x_s.at[i, n, core], x_r.at[i, j, core], x_ss, x_rs.at[i + 3 * half], dev(x=n))

    with scope("hear3"):
        hear(3)
    for k, (i, half) in enumerate([(0, 0), (0, 1), *halves]):
        r = label((zl + 4 - (0, *ALONG)[i]) % 4)
        core = (c + half) % 2
        if k != 1:
            with scope(f"x_wait{i}{half}"):
                landed = x_r.at[i, :, core] if i else x_r.at[0]
                bytes_of(landed, x_ss, x_rs.at[i + 3 * half]).wait_recv()
        total = x_own[i, x, core]
        for j in range(3):
            total = total + decode(x_r[i, j, core])
        g_s[i, core] = encode(total)
        to = (g_s.at[i, core], g_r.at[zh, c], g_ss.at[half], g_rs.at[zh], dev(zl=r, c=core, zh=group))
        if half:
            send(*to)
        else:
            here = jnp.logical_and(r == zl, zh == group)

            @pl.when(here)
            def _():
                g_r[zh, c] = g_s[i, core]

            @pl.when(jnp.logical_not(here))
            def _():
                send(*to)

    with scope("left"):
        for ref, sem in (
            (core_r, core_ss), (y_r, y_ss), (z_r, z_ss), (a_all.at[:, 0], ca_ss), (z_r, yb_ss), (z_r, za_ss), (x_r, x_ss)
        ):
            bytes_of(ref, sem, z_rs).wait_send()

    total = [jnp.zeros((64, 128), F32)] * 2
    for a in range(4):
        here = jnp.logical_and(holder(zh, a) == zl, zh == a)

        @pl.when(here)
        def _():
            bytes_of(g_r.at[a, 0], g_ss.at[0], g_rs.at[a]).wait_recv()

        @pl.when(jnp.logical_not(here))
        def _():
            with scope(f"g_wait{a}"):
                bytes_of(g_r.at[a], g_ss.at[0], g_rs.at[a]).wait_recv()

        for core in range(2):
            total[core] = total[core] + decode(g_r[a, core])
    first, second = total[0] * 2.0**-32, total[1] * 2.0**-32
    out[0] = jnp.where(lane < 64, first, pltpu.roll(second, 64, 1))
    out[1] = jnp.where(lane < 64, pltpu.roll(first, 64, 1), second)

    bytes_of(g_s.at[:, 0], g_ss.at[1], z_rs).wait_send()
    here = group == zh

    @pl.when(here)
    def _():
        bytes_of(g_s.at[0:3, 0], g_ss.at[0], z_rs).wait_send()

    @pl.when(jnp.logical_not(here))
    def _():
        bytes_of(g_s.at[:, 0], g_ss.at[0], z_rs).wait_send()


def per_device(coefficients, exponent, amplitude, centers, momenta, quad_weight):
    vmem, dma = pltpu.VMEM, pltpu.SemaphoreType.DMA
    return pl.pallas_call(
        kernel,
        out_shape=pltpu.VMEM((2, 64, 128), F32),
        in_specs=[pl.BlockSpec(memory_space=pl.ANY)] * 6,
        out_specs=pl.BlockSpec(memory_space=pltpu.VMEM),
        scratch_shapes=[
            vmem((4, 4, 2, 64, 1024), BF16), vmem((1, 1024), F32), vmem((1, 1024), F32), vmem((3, 1024), F32),
            vmem((3, 192), F32), vmem((1, 192), F32), vmem((8, 256), F32), vmem((256, 8), F32),
            vmem((384, 1024), BF16),
            vmem((4, 4, 64, 384), F32), vmem((4, 4, 64, 384), BF16), vmem((4, 4, 64, 384), BF16),
            vmem((4, 4, 64, 384), BF16), vmem((4, 3, 64, 384), BF16),
            vmem((3, 64, 384), BF16), vmem((3, 64, 384), BF16), vmem((64, 384), BF16),
            vmem((4, 2, 64, 384), BF16), vmem((4, 2, 64, 384), BF16),
            vmem((4, 4, 2, 64, 128), BF16), vmem((4, 4, 2, 64, 128), F32), vmem((4, 3, 2, 64, 128), BF16),
            vmem((4, 2, 64, 128), BF16), vmem((4, 2, 64, 128), BF16),
            dma((5,)), dma((4,)), pltpu.SemaphoreType.REGULAR((4,)),
            dma, dma((4,)), dma, dma((8,)), dma, dma, dma, dma((4,)), dma, dma((3,)), dma, dma((3,)),
            dma, dma((7,)), dma((2,)), dma((4,)),
        ],
        compiler_params=pltpu.CompilerParams(
            collective_id=0, has_side_effects=True, vmem_limit_bytes=60 * 1024 * 1024
        ),
        name="scattering",
    )(
        coefficients.reshape(4, 4, 2, 64, 1024),
        exponent.reshape(1, 1024),
        amplitude.reshape(1, 1024),
        centers,
        momenta,
        quad_weight.reshape(1, 192),
    )


def solution(mesh):
    return jax.shard_map(
        per_device,
        mesh=mesh,
        in_specs=(P(None, "pair"), P("pair"), P("pair"), P(None, "pair"), P(None, "mom"), P("mom")),
        out_specs=P(None, "pair", "mom"),
        check_vma=False,
    )
```

```python
import math

import jax
import jax.numpy as jnp
from jax import lax
from jax.experimental import pallas as pl
from jax.experimental.pallas import tpu as pltpu
from jax.sharding import PartitionSpec as P

MESH = pl.DeviceIdType.MESH
scope = jax.named_scope
BF16, F32 = jnp.bfloat16, jnp.float32
NT = (((1,), (1,)), ((), ()))

RING = (2, 1, 3)
NEAR = (1, 3, 2)
ALL, LOW, HIGH = pl.ds(0, 64), pl.ds(0, 32), pl.ds(32, 32)
PARTS = ((ALL,), (ALL,), (LOW, HIGH), (ALL,))
ALONG = (3, 2, 1)
LINE = (2, 1, 3, 0)


def _fit(values, degree):
    import numpy as np

    nodes = 0.125 * (1.0 - np.cos(np.pi * (np.arange(400) + 0.5) / 400))
    weights = np.polynomial.chebyshev.chebfit(8.0 * nodes - 1.0, values(nodes), degree)
    series = np.polynomial.Chebyshev(weights, domain=[0.0, 0.25])
    return [float(c) for c in series.convert(kind=np.polynomial.Polynomial).coef]


def _sin_over(v):
    import numpy as np

    u = np.sqrt(v)
    return math.sqrt(2.0) * np.sin(np.pi * u) / u


def _cos_of(v):
    import numpy as np

    return -math.sqrt(2.0) * np.cos(np.pi * np.sqrt(v))


SIN_C = _fit(_sin_over, 4)
COS_C = _fit(_cos_of, 4)


def horner(coefs, v):
    total = coefs[-1] * v + coefs[-2]
    for c in coefs[-3::-1]:
        total = total * v + c
    return total


def encode(x):
    return (x * jnp.abs(x)).astype(BF16)


def decode(y):
    y = y.astype(F32)
    return y * lax.rsqrt(jnp.maximum(jnp.abs(y), 1e-37))


def kernel(
    coef_h, expo_h, amp_h, cen_h, mom_h, qw_h, out,
    coef_v, expo_v, amp_v, cen_v, mom_v, qw_v, rows_v, cols_v, integ,
    prod, core_s, core_r, y_s, y_r, z_s, z_r, r_own, b_all, a_all,
    x_s, x_own, x_r, g_s, g_r,
    in_sem, coef_sem, heard,
    core_ss, core_rs, y_ss, y_rs, z_ss, z_rs, ca_ss, ca_rs, yb_ss, yb_rs, za_ss, za_rs,
    x_ss, x_rs, g_ss, g_rs,
):
    pair, mom = lax.axis_index("pair"), lax.axis_index("mom")
    y, zl, c = pair // 8, (pair // 2) % 4, pair % 2
    x, zh = mom // 4, mom % 4
    z = zh * 4 + zl

    def label(zl):
        return (zl + 3 - 2 * (zh // 2)) % 4

    def holder(group, window):
        return (group + 1 + 2 * (window // 2)) % 4

    group = label(zl)

    def dev(y=y, zl=zl, c=c, x=x, zh=zh):
        return {"pair": y * 8 + zl * 2 + c, "mom": x * 4 + zh}

    def each_way(k, act):
        for step in (2**k, -(2**k)):
            far = z + step

            @pl.when(jnp.logical_and(far >= 0, far < 16))
            def _():
                act(far)

    def ways(k):
        return (z + 16 - 2**k) // 16 + (31 - z - 2**k) // 16

    def tell(k):
        def act(far):
            to = dev(zl=far % 4, zh=far // 4)
            pl.semaphore_signal(heard.at[k], inc=1, device_id=to, device_id_type=MESH)

        each_way(k, act)

    def hear(k):
        pl.semaphore_wait(heard.at[k], ways(k))

    def send(src, dst, ss, rs, to):
        copy = pltpu.make_async_remote_copy(
            src_ref=src, dst_ref=dst, send_sem=ss, recv_sem=rs, device_id=to, device_id_type=MESH
        )
        copy.start()
        return copy

    def bytes_of(ref, ss, rs):
        return pltpu.make_async_remote_copy(
            src_ref=ref, dst_ref=ref, send_sem=ss, recv_sem=rs, device_id=dev(c=1 - c), device_id_type=MESH
        )

    small = [
        pltpu.make_async_copy(h, v, in_sem.at[i])
        for i, (h, v) in enumerate(
            [(expo_h, expo_v), (amp_h, amp_v), (cen_h, cen_v), (mom_h, mom_v), (qw_h, qw_v)]
        )
    ]
    for copy in small:
        copy.start()
    barrier = pltpu.get_barrier_semaphore()
    near = [dev(c=1 - c)]
    near += [dev(y=(y + d) % 4) for d in RING]
    near += [dev(zl=(zl + d) % 4) for d in (1, 2, 3)]
    near += [dev(x=(x + d) % 4) for d in RING]
    for to in near:
        pl.semaphore_signal(barrier, inc=1, device_id=to, device_id_type=MESH)

    def greet(far):
        @pl.when(far // 4 != zh)
        def _():
            to = dev(zl=far % 4, zh=far // 4)
            pl.semaphore_signal(barrier, inc=1, device_id=to, device_id_type=MESH)

    each_way(0, greet)
    greeted = len(near) + (3 - zl) // 3 * ((zh + 3) // 4) + zl // 3 * ((6 - zh) // 4)

    coef_in = []
    for t in range(4):
        copy = pltpu.make_async_copy(coef_h.at[:, label((zl + LINE[t]) % 4)], coef_v.at[t], coef_sem.at[t])
        copy.start()
        coef_in.append(copy)

    with scope("small_wait"):
        for copy in small:
            copy.wait()
    m = mom_v[...]
    squared = m[0:1] * m[0:1] + m[1:2] * m[1:2] + m[2:3] * m[2:3]
    rows_v[...] = jnp.zeros_like(rows_v)
    rows_v[0:3, 0:192] = m
    rows_v[3:4, 0:192] = squared
    rows_v[4:5, 0:192] = jnp.sqrt(qw_v[...] / (3072.0 * (0.5 * squared + 0.5)))
    cols_v[...] = jnp.transpose(rows_v[...])
    cen_v[...] = cen_v[...] * (0.5 / math.pi)
    expo_v[...] = (-0.25 / math.log(2.0)) / expo_v[...]

    def integrals(i, carry):
        base = pl.multiple_of(i * 16, 16)
        k = cols_v[pl.ds(base, 16), :]
        first = i < 8
        row_c = pl.multiple_of(jnp.where(first, base, base + 128), 16)
        row_s = pl.multiple_of(jnp.where(first, base + 128, base + 192), 16)
        for start in range(0, 1024, 256):
            p = slice(start, start + 256)
            turns = cen_v[0:1, p] * k[:, 0:1] + cen_v[1:2, p] * k[:, 1:2] + cen_v[2:3, p] * k[:, 2:3]
            u = turns - jnp.round(turns)
            v = u * u
            s = horner(SIN_C, v) * u
            envelope = (amp_v[:, p] * jnp.exp2(k[:, 3:4] * expo_v[:, p])) * k[:, 4:5]
            product = envelope * s
            integ[pl.ds(row_c, 16), p] = (envelope - product * s).astype(BF16)
            integ[pl.ds(row_s, 16), p] = (product * horner(COS_C, v)).astype(BF16)
        return carry

    with scope("integrals"):
        lax.fori_loop(0, 12, integrals, 0, unroll=12)


    def half(t, core):
        rows = coef_v[t, :, core].reshape(256, 1024)
        return lax.dot_general(rows, integ[...], NT, preferred_element_type=F32).reshape(4, 64, 384)

    def contract(t):
        with scope(f"coef_wait{t}"):
            coef_in[t].wait()
        core_s[t] = encode(half(t, 1 - c))
        if t == 0:
            with scope("barrier"):
                pl.semaphore_wait(barrier, greeted)
            tell(0)
        send(core_s.at[t], core_r.at[t], core_ss, core_rs.at[t], dev(c=1 - c))
        prod[t] = half(t, c)

    def spread(t):
        with scope(f"core_wait{t}"):
            bytes_of(core_r.at[t], core_ss, core_rs.at[t]).wait_recv()
        total = prod[t] + decode(core_r[t])
        prod[t] = total
        y_s[t] = encode(total)
        for k, rows in enumerate(PARTS[t]):
            for i, d in enumerate(RING):
                to = dev(y=(y + d) % 4)
                send(y_s.at[t, (y + d) % 4, rows], y_r.at[t, i, rows], y_ss, y_rs.at[t + 2 * k], to)

    contract(0)
    contract(1)
    for t in range(4):
        spread(t)
        if t < 2:
            contract(t + 2)
        if t == 1:
            hear(0)
            tell(1)
        if t == 3:
            hear(1)
            tell(2)

    for t in range(4):
        for k, rows in enumerate(PARTS[t]):
            with scope(f"y_wait{t}{k}"):
                bytes_of(y_r.at[t, :, rows], y_ss, y_rs.at[t + 2 * k]).wait_recv()
            total = prod[t, y, rows]
            for i in range(3):
                total = total + decode(y_r[t, i, rows])
            if t < 3:
                z_s[t, rows] = encode(total)
                send(z_s.at[t, rows], z_r.at[t, rows], z_ss, z_rs, dev(zl=(zl + LINE[t]) % 4))
        if t == 2:
            hear(2)
            tell(3)

    with scope("z_wait"):
        bytes_of(z_r, z_ss, z_rs).wait_recv()
    for t in range(3):
        total = total + decode(z_r[t])
    r_own[...] = (total * 65536.0).astype(BF16)

    ca = [send(r_own, a_all.at[group, c], ca_ss, ca_rs.at[0], dev(c=1 - c))]
    yb = [
        send(r_own, b_all.at[y, 0], yb_ss, yb_rs.at[i], dev(y=(y + d) % 4)) for i, d in enumerate(NEAR)
    ]
    za = [
        send(r_own, a_all.at[group, c], za_ss, za_rs.at[i], dev(zl=(zl + d) % 4)) for i, d in enumerate(ALONG)
    ]
    lane = lax.broadcasted_iota(jnp.int32, (64, 128), 1)

    def turn(n):
        rows = b_all[n, 0].astype(F32)
        last = pltpu.roll(rows[:, 256:384], 64, 1) * jnp.where(lane < 64, 1.0, -1.0)
        b_all[n, 1] = jnp.concatenate([rows[:, 128:256], -rows[:, 0:128], last], axis=1).astype(BF16)

    b_all[y, 0] = r_own[...]
    a_all[group, c] = r_own[...]
    x_c = []
    with scope("ca_wait0"):
        ca[0].wait_recv()
    left = a_all[group].reshape(128, 384)
    def forward(i):
        with scope(f"za_wait{i}"):
            za[i].wait_recv()
        here = a_all.at[label((zl + 4 - ALONG[i]) % 4), c]
        ca.append(send(here, here, ca_ss, ca_rs.at[i + 1], dev(c=1 - c)))

    for i, d in enumerate((0, *NEAR)):
        n = (y + 4 - d) % 4
        if d:
            with scope(f"yb_wait{i}"):
                yb[i - 1].wait_recv()
        turn(n)
        block = lax.dot_general(left, b_all[n].reshape(128, 384), NT, preferred_element_type=F32)
        x_own[0, n] = block.reshape(2, 64, 128)
        x_s[0, n] = encode(block).reshape(2, 64, 128)
        e = (n - x + 4) % 4

        @pl.when(e > 0)
        def _():
            send(x_s.at[0, n], x_r.at[0, e - 1], x_ss, x_rs.at[0], dev(x=n))

        if d:
            forward(i - 1)

    halves = [(i, half) for half in range(2) for i in range(1, 4)]
    for i, half in halves:
        core = (c + half) % 2
        if half:
            with scope(f"ca_wait{i}"):
                ca[i].wait_recv()
        left = a_all[label((zl + 4 - (0, *ALONG)[i]) % 4), core]
        block = lax.dot_general(left, b_all[...].reshape(512, 384), NT, preferred_element_type=F32)
        for n in range(4):
            x_own[i, n, core] = block[:, n * 128 : n * 128 + 128]
            x_s[i, n, core] = encode(block[:, n * 128 : n * 128 + 128])
        for j, e in enumerate(RING):
            n = (x + e) % 4
            send(x_s.at[i, n, core], x_r.at[i, j, core], x_ss, x_rs.at[i + 3 * half], dev(x=n))

    with scope("hear3"):
        hear(3)
    for k, (i, half) in enumerate([(0, 0), (0, 1), *halves]):
        r = label((zl + 4 - (0, *ALONG)[i]) % 4)
        core = (c + half) % 2
        if k != 1:
            with scope(f"x_wait{i}{half}"):
                landed = x_r.at[i, :, core] if i else x_r.at[0]
                bytes_of(landed, x_ss, x_rs.at[i + 3 * half]).wait_recv()
        total = x_own[i, x, core]
        for j in range(3):
            total = total + decode(x_r[i, j, core])
        g_s[i, core] = encode(total)
        to = (g_s.at[i, core], g_r.at[zh, c], g_ss.at[half], g_rs.at[zh], dev(zl=r, c=core, zh=group))
        if half:
            send(*to)
        else:
            here = jnp.logical_and(r == zl, zh == group)

            @pl.when(here)
            def _():
                g_r[zh, c] = g_s[i, core]

            @pl.when(jnp.logical_not(here))
            def _():
                send(*to)

    with scope("left"):
        for ref, sem in (
            (core_r, core_ss), (y_r, y_ss), (z_r, z_ss), (a_all.at[:, 0], ca_ss), (z_r, yb_ss), (z_r, za_ss), (x_r, x_ss)
        ):
            bytes_of(ref, sem, z_rs).wait_send()

    total = [jnp.zeros((64, 128), F32)] * 2
    for a in range(4):
        here = jnp.logical_and(holder(zh, a) == zl, zh == a)

        @pl.when(here)
        def _():
            bytes_of(g_r.at[a, 0], g_ss.at[0], g_rs.at[a]).wait_recv()

        @pl.when(jnp.logical_not(here))
        def _():
            with scope(f"g_wait{a}"):
                bytes_of(g_r.at[a], g_ss.at[0], g_rs.at[a]).wait_recv()

        for core in range(2):
            total[core] = total[core] + decode(g_r[a, core])
    first, second = total[0] * 2.0**-32, total[1] * 2.0**-32
    out[0] = jnp.where(lane < 64, first, pltpu.roll(second, 64, 1))
    out[1] = jnp.where(lane < 64, pltpu.roll(first, 64, 1), second)

    bytes_of(g_s.at[:, 0], g_ss.at[1], z_rs).wait_send()
    here = group == zh

    @pl.when(here)
    def _():
        bytes_of(g_s.at[0:3, 0], g_ss.at[0], z_rs).wait_send()

    @pl.when(jnp.logical_not(here))
    def _():
        bytes_of(g_s.at[:, 0], g_ss.at[0], z_rs).wait_send()


def per_device(coefficients, exponent, amplitude, centers, momenta, quad_weight):
    vmem, dma = pltpu.VMEM, pltpu.SemaphoreType.DMA
    return pl.pallas_call(
        kernel,
        out_shape=pltpu.VMEM((2, 64, 128), F32),
        in_specs=[pl.BlockSpec(memory_space=pl.ANY)] * 6,
        out_specs=pl.BlockSpec(memory_space=pltpu.VMEM),
        scratch_shapes=[
            vmem((4, 4, 2, 64, 1024), BF16), vmem((1, 1024), F32), vmem((1, 1024), F32), vmem((3, 1024), F32),
            vmem((3, 192), F32), vmem((1, 192), F32), vmem((8, 256), F32), vmem((256, 8), F32),
            vmem((384, 1024), BF16),
            vmem((4, 4, 64, 384), F32), vmem((4, 4, 64, 384), BF16), vmem((4, 4, 64, 384), BF16),
            vmem((4, 4, 64, 384), BF16), vmem((4, 3, 64, 384), BF16),
            vmem((3, 64, 384), BF16), vmem((3, 64, 384), BF16), vmem((64, 384), BF16),
            vmem((4, 2, 64, 384), BF16), vmem((4, 2, 64, 384), BF16),
            vmem((4, 4, 2, 64, 128), BF16), vmem((4, 4, 2, 64, 128), F32), vmem((4, 3, 2, 64, 128), BF16),
            vmem((4, 2, 64, 128), BF16), vmem((4, 2, 64, 128), BF16),
            dma((5,)), dma((4,)), pltpu.SemaphoreType.REGULAR((4,)),
            dma, dma((4,)), dma, dma((5,)), dma, dma, dma, dma((4,)), dma, dma((3,)), dma, dma((3,)),
            dma, dma((7,)), dma((2,)), dma((4,)),
        ],
        compiler_params=pltpu.CompilerParams(
            collective_id=0, has_side_effects=True, vmem_limit_bytes=60 * 1024 * 1024
        ),
        name="scattering",
    )(
        coefficients.reshape(4, 4, 2, 64, 1024),
        exponent.reshape(1, 1024),
        amplitude.reshape(1, 1024),
        centers,
        momenta,
        quad_weight.reshape(1, 192),
    )


def solution(mesh):
    return jax.shard_map(
        per_device,
        mesh=mesh,
        in_specs=(P(None, "pair"), P("pair"), P("pair"), P(None, "pair"), P(None, "mom"), P("mom")),
        out_specs=P(None, "pair", "mom"),
        check_vma=False,
    )
```
